32 devices in a mesh: row: 16 (over z, x, core), col: 2 (over y).
Axes of the slice: x: 2, y: 2, z: 4, core: 2. Of those that a mesh axis runs over, the one named last changes fastest.
Arguments:
- tokens: bfloat16 [32768, 1024], P('row', 'col'), may hold values from -6 to 6
- qkv_weight: bfloat16 [1024, 3, 1024], P('row', None, 'col'), may hold values from -0.25 to 0.25
- qv_bias: float32 [2, 1024], P(None, 'col'), may hold values from -3 to 3
- out_weight: bfloat16 [1024, 1024], P('row', 'col'), may hold values from -0.75 to 0.75
- out_bias: float32 [1024], P('col'), may hold values from -3 to 3
- norm1_gain: float32 [1024], P('col'), may hold values from 0.1 to 1.9
- norm1_shift: float32 [1024], P('col'), may hold values from -3 to 3
- in_weight: bfloat16 [1024, 4096], P('row', 'col'), may hold values from -0.1875 to 0.1875
- in_bias: float32 [4096], P('col'), may hold values from -3 to 3
- down_weight: bfloat16 [1024, 4096], P('row', 'col'), may hold values from -0.1875 to 0.1875
- down_bias: float32 [1024], P('col'), may hold values from -3 to 3
- norm2_gain: float32 [1024], P('col'), may hold values from 0.1 to 1.9
- norm2_shift: float32 [1024], P('col'), may hold values from -3 to 3
- lengths: int32 [64], P('row'), may hold values from 128 to 512, as said below
- cotangent: bfloat16 [32768, 1024], P('row', 'col'), may hold values from -6 to 6
Outputs:
- layer_out: bfloat16 [32768, 1024], P('row', 'col')
- tokens_grad: float32 [32768, 1024], P('row', 'col')
- qkv_weight_grad: float32 [1024, 3, 1024], P('row', None, 'col')
- qv_bias_grad: float32 [2, 1024], P(None, 'col')
- out_weight_grad: float32 [1024, 1024], P('row', 'col')
- out_bias_grad: float32 [1024], P('col')
- norm1_gain_grad: float32 [1024], P('col')
- norm1_shift_grad: float32 [1024], P('col')
- in_weight_grad: float32 [1024, 4096], P('row', 'col')
- in_bias_grad: float32 [4096], P('col')
- down_weight_grad: float32 [1024, 4096], P('row', 'col')
- down_bias_grad: float32 [1024], P('col')
- norm2_gain_grad: float32 [1024], P('col')
- norm2_shift_grad: float32 [1024], P('col')
The draws below stay inside these ranges and needn't reach their ends.
Inputs may be any that keep to these rules, and one draw needn't show every extreme that they name: `lengths`: the valid tokens of each sequence come first; in every draw some sequence has all 512 tokens valid.
All inputs are finite; a program needn't handle non-finite values.
Results may differ from the reference program's by a relative error of at most 0.02.
Values may be sent and summed in bfloat16 or wider, within the bound.
No kernel may reach another device: no remote copies, remote signals or barrier semaphores. Data moves between devices by JAX's collectives and lax.ppermute only.
A program may use at most 192 MiB of HBM per device.

```python
import jax
import jax.numpy as jnp
from jax import lax

D = 1024
HEADS = 16
FF = 4096
HEAD_DIM = 64
SEQ_LEN = 512
SEQ_ROW = 4
TOK_ROW = 2048
SEQS = 64
TOKENS = 32768
N_ROW = 16


def draw_lengths(key, part):
    key = jax.random.fold_in(key, 7)
    first_key, second_key = jax.random.split(key)
    counts = jax.random.randint(first_key, (SEQS,), SEQ_LEN // 4, SEQ_LEN + 1)
    chosen = jax.random.randint(second_key, (), 0, SEQS)
    return jnp.where(jnp.arange(SEQS) == chosen, SEQ_LEN, counts).astype(jnp.int32)


def steps_of(rng, shape, pieces, low, largest):
    def one(dim, shards_of):
        heights = jax.random.uniform(jax.random.fold_in(jax.random.fold_in(rng, 6), dim), (shards_of,), jnp.float32, low / len(pieces), largest / len(pieces))
        return jnp.repeat(jnp.exp(heights), shape[dim] // shards_of).reshape((-1,) + (1,) * (len(shape) - dim - 1))

    loudness = one(*pieces[0])
    for cut in pieces[1:]:
        loudness = loudness * one(*cut)
    return loudness


def scatter_about(key, extent, scale, bound, shards=(), held_as=jnp.bfloat16):
    array = jax.random.normal(key, extent, jnp.float32) * scale
    if len(shards) > 0:
        array = steps_of(key, extent, shards, -0.22, 0.18) * array
    return jnp.clip(array, min=-bound, max=bound).astype(held_as)


def setup_inputs(seed: int = 0) -> dict:
    key_of = jax.random.split(jax.random.key(seed), 16)
    return {
        "tokens": scatter_about(key_of[0], (TOKENS, D), 1.0, 6.0, ((0, 16), (1, 2))),
        "qkv_weight": scatter_about(key_of[1], (D, 3, D), (D // 2) ** -0.5, 0.25, ((0, 16), (2, 2))),
        "qv_bias": scatter_about(key_of[2], (2, D), 0.5, 3.0, ((1, 2),), jnp.float32),
        "out_weight": scatter_about(key_of[3], (D, D), (D // 16) ** -0.5, 0.75, ((0, 16), (1, 2))),
        "out_bias": scatter_about(key_of[4], (D,), 0.5, 3.0, ((0, 2),), jnp.float32),
        "norm1_gain": jnp.clip(1.0 + 0.18 * jax.random.normal(key_of[5], (D,), jnp.float32), 0.1, 1.9),
        "norm1_shift": scatter_about(key_of[6], (D,), 0.5, 3.0, ((0, 2),), jnp.float32),
        "in_weight": scatter_about(key_of[7], (D, FF), D ** -0.5, 0.1875, ((0, 16), (1, 2))),
        "in_bias": scatter_about(key_of[8], (FF,), 0.5, 3.0, ((0, 2),), jnp.float32),
        "down_weight": scatter_about(key_of[9], (D, FF), (FF // 4) ** -0.5, 0.1875, ((0, 16), (1, 2))),
        "down_bias": scatter_about(key_of[10], (D,), 0.5, 3.0, ((0, 2),), jnp.float32),
        "norm2_gain": jnp.clip(1.0 + 0.18 * jax.random.normal(key_of[11], (D,), jnp.float32), 0.1, 1.9),
        "norm2_shift": scatter_about(key_of[12], (D,), 0.5, 3.0, ((0, 2),), jnp.float32),
        "lengths": draw_lengths(jax.random.fold_in(key_of[15], 71), 0),
        "cotangent": scatter_about(key_of[14], (TOKENS, D), 1.0, 6.0, ((0, 16), (1, 2))),
    }


@jax.custom_vjp
def low(v):
    return lax.optimization_barrier(v.astype(jnp.bfloat16)).astype(jnp.float32)

@jax.custom_vjp
def low_back(v):
    return v

def low_keep(v):
    return (low(v), None)

def low_pass(kept, grad):
    return (grad,)

def back_keep(v):
    return (v, None)

def back_low(kept, grad):
    return (low(grad),)
low.defvjp(low_keep, low_pass)
low_back.defvjp(back_keep, back_low)
epsilon = 1e-05
masked_score = -1000000000.0
highest = lax.Precision.HIGHEST

def layer_norm(summed, norm_gain, norm_shift):
    center = lax.optimization_barrier(jnp.mean(summed, axis=-1, keepdims=True))
    shifted = summed - center
    spread = lax.optimization_barrier(jnp.mean(shifted * shifted, axis=-1, keepdims=True))
    return shifted * lax.rsqrt(spread + epsilon) * norm_gain + norm_shift

def attend(element):
    queries, key_rows, values, length = element
    factor = HEAD_DIM ** (-0.5)
    scores = jnp.einsum('qhd,khd->hqk', queries, key_rows, precision=highest) * factor
    scores = low_back(scores)
    usable = jnp.arange(SEQ_LEN) < length
    scores = jnp.where(usable[None, None, :], scores, masked_score)
    chances = jax.nn.softmax(scores, axis=-1)
    context = jnp.einsum('hqk,khd->qhd', low(chances), values, precision=highest)
    return low(low_back(context))

def block(rows, params, group_lengths):
    qkv_weight, qv_bias, out_weight, out_bias, norm1_gain, norm1_shift, in_weight, in_bias, down_weight, down_bias, norm2_gain, norm2_shift = params
    projected = jnp.einsum('td,dsf->tsf', rows, qkv_weight, precision=highest)
    qkv_bias = jnp.stack([qv_bias[0], jnp.zeros_like(qv_bias[0]), qv_bias[1]])
    qkv_rows = low(low_back(projected + qkv_bias))
    split_rows = qkv_rows.reshape(SEQ_ROW, SEQ_LEN, 3, HEADS, HEAD_DIM)
    context = lax.map(jax.checkpoint(attend), (split_rows[:, :, 0], split_rows[:, :, 1], split_rows[:, :, 2], group_lengths))
    context = context.reshape(TOK_ROW, D)
    attended = low_back(jnp.dot(context, out_weight.T, precision=highest) + out_bias)
    hidden_one = layer_norm(rows + attended, norm1_gain, norm1_shift)
    pre_act = low_back(jnp.dot(low(hidden_one), in_weight, precision=highest) + in_bias)
    activated = low(jax.nn.gelu(pre_act, approximate=False))
    fed = low_back(jnp.dot(activated, down_weight.T, precision=highest) + down_bias)
    return layer_norm(hidden_one + fed, norm2_gain, norm2_shift)

def reference(tokens, qkv_weight, qv_bias, out_weight, out_bias, norm1_gain, norm1_shift, in_weight, in_bias, down_weight, down_bias, norm2_gain, norm2_shift, lengths, cotangent):
    params = (qkv_weight.astype(jnp.float32), qv_bias.astype(jnp.float32), out_weight.astype(jnp.float32), out_bias.astype(jnp.float32), norm1_gain.astype(jnp.float32), norm1_shift.astype(jnp.float32), in_weight.astype(jnp.float32), in_bias.astype(jnp.float32), down_weight.astype(jnp.float32), down_bias.astype(jnp.float32), norm2_gain.astype(jnp.float32), norm2_shift.astype(jnp.float32))
    token_groups = tokens.astype(jnp.float32).reshape(N_ROW, TOK_ROW, D)
    upstream_groups = cotangent.astype(jnp.float32).reshape(N_ROW, TOK_ROW, D)
    length_groups = lengths.reshape(N_ROW, SEQ_ROW)

    def group_step(totals, element):
        rows, upstream, group_lengths = element

        def forward(rows_in, params_in):
            return block(rows_in, params_in, group_lengths)
        output, pullback = jax.vjp(forward, rows, params)
        row_grad, param_grads = pullback(upstream)
        totals = jax.tree.map(jnp.add, totals, param_grads)
        return (totals, (output.astype(jnp.bfloat16), row_grad))
    zeros = jax.tree.map(jnp.zeros_like, params)
    totals, (outputs, row_grads) = lax.scan(group_step, zeros, (token_groups, upstream_groups, length_groups))
    return (outputs.reshape(TOKENS, D), row_grads.reshape(TOKENS, D), totals[0], totals[1], totals[2], totals[3], totals[4], totals[5], totals[6], totals[7], totals[8], totals[9], totals[10], totals[11])
```

```python
import jax
import jax.numpy as jnp
from jax import lax
from jax.experimental import pallas as pl
from jax.experimental.pallas import tpu as pltpu
from jax.sharding import PartitionSpec as P

HEAD_DIM = 64
SEQ_LEN = 512


epsilon = 1e-05
masked_score = -1000000000.0


def widen(portion):
    return lax.all_gather(portion, "col", axis=1, tiled=True)


def widen_grad(portion):
    return lax.all_gather(portion, "col", axis=1, tiled=True)


def reduce_out(partial_rows):
    return lax.psum_scatter(partial_rows, "col", scatter_dimension=1, tiled=True)


def reduce_grad(partial_rows):
    return lax.psum_scatter(partial_rows, "col", scatter_dimension=1, tiled=True)


def exact_gelu(values):
    return jax.nn.gelu(values, approximate=False)


def normalize(summed, norm_gain, norm_shift, features):
    moments = lax.psum((jnp.sum(summed, 1), jnp.sum(summed * summed, 1)), "col")
    center = moments[0] / features
    inverse = lax.rsqrt(moments[1] / features - center * center + epsilon)
    normal = (summed - center[:, None]) * inverse[:, None]
    return (normal * norm_gain + norm_shift, normal, inverse)


def normalize_back(gradient, normal, inverse, norm_gain, features):
    scaled = gradient * norm_gain
    moments = lax.psum((jnp.sum(scaled, 1), jnp.sum(scaled * normal, 1)), "col")
    return inverse[:, None] * (
        scaled - moments[0][:, None] / features - normal * moments[1][:, None] / features
    )


def masked_scores(queries, key_rows, length):
    factor = HEAD_DIM ** (-0.5)
    scores = (
        jnp.einsum("qhd,khd->hqk", queries, key_rows, preferred_element_type=jnp.float32) * factor
    )
    usable = jnp.arange(scores.shape[2]) < length
    return jnp.where(usable[None, None, :], scores, masked_score)


def attend_forward(element):
    queries, key_rows, values, length = element
    scores = masked_scores(queries, key_rows, length)
    highest = jnp.max(scores, 2, keepdims=True)
    raised = jnp.exp(scores - highest)
    row_total = jnp.sum(raised, 2, keepdims=True)
    chances = (raised / row_total).astype(jnp.bfloat16)
    context = jnp.einsum("hqk,khd->qhd", chances, values, preferred_element_type=jnp.float32)
    return (context.astype(jnp.bfloat16), (highest + jnp.log(row_total))[:, :, 0])


def attend_back(element):
    queries, key_rows, values, context_grad, logsum, length = element
    factor = HEAD_DIM ** (-0.5)
    scores = masked_scores(queries, key_rows, length)
    chances = jnp.exp(scores - logsum[:, :, None])
    chance_grad = jnp.einsum(
        "qhd,khd->hqk", context_grad, values, preferred_element_type=jnp.float32
    )
    value_grad = jnp.einsum(
        "hqk,qhd->khd",
        chances.astype(jnp.bfloat16),
        context_grad,
        preferred_element_type=jnp.float32,
    )
    inner = jnp.sum(chances * chance_grad, 2, keepdims=True)
    score_grad = (chances * (chance_grad - inner)).astype(jnp.bfloat16)
    query_grad = (
        jnp.einsum("hqk,khd->qhd", score_grad, key_rows, preferred_element_type=jnp.float32)
        * factor
    )
    key_grad = (
        jnp.einsum("hqk,qhd->khd", score_grad, queries, preferred_element_type=jnp.float32) * factor
    )
    return jnp.stack([query_grad, key_grad, value_grad], 1).astype(jnp.bfloat16)


def on_device(
    tokens,
    qkv_weight,
    qv_bias,
    out_weight,
    out_bias,
    norm1_gain,
    norm1_shift,
    in_weight,
    in_bias,
    down_weight,
    down_bias,
    norm2_gain,
    norm2_shift,
    lengths,
    cotangent,
):
    local_width = tokens.shape[1]
    features = local_width * lax.axis_size("col")
    token_count = tokens.shape[0]
    sequences = lengths.shape[0]
    heads_here = local_width // HEAD_DIM
    qkv_full, out_full, in_full, down_full = (
        lax.all_gather(qkv_weight, "row", axis=0, tiled=True),
        lax.all_gather(out_weight, "row", axis=0, tiled=True),
        lax.all_gather(in_weight, "row", axis=0, tiled=True),
        lax.all_gather(down_weight, "row", axis=0, tiled=True),
    )
    tokens_full = widen(tokens)
    projected = jnp.einsum("td,dsf->tsf", tokens_full, qkv_full, preferred_element_type=jnp.float32)
    qkv_bias = jnp.stack([qv_bias[0], jnp.zeros_like(qv_bias[0]), qv_bias[1]])
    qkv_rows = (projected + qkv_bias).astype(jnp.bfloat16)
    split_rows = qkv_rows.reshape(sequences, SEQ_LEN, 3, heads_here, HEAD_DIM)
    queries = split_rows[:, :, 0]
    key_rows = split_rows[:, :, 1]
    values = split_rows[:, :, 2]
    context, logsums = lax.map(attend_forward, (queries, key_rows, values, lengths))
    context = context.reshape(token_count, local_width)
    attended = (
        reduce_out(jnp.einsum("tf,of->to", context, out_full, preferred_element_type=jnp.float32))
        + out_bias
    )
    first_sum = tokens.astype(jnp.float32) + attended
    hidden_one, normal_one, inverse_one = normalize(first_sum, norm1_gain, norm1_shift, features)
    hidden_low = hidden_one.astype(jnp.bfloat16)
    hidden_full = widen(hidden_low)
    pre_act = jnp.dot(hidden_full, in_full, preferred_element_type=jnp.float32) + in_bias
    activated = exact_gelu(pre_act).astype(jnp.bfloat16)
    fed = (
        reduce_out(
            jnp.einsum("tf,of->to", activated, down_full, preferred_element_type=jnp.float32)
        )
        + down_bias
    )
    second_sum = hidden_one + fed
    output, normal_two, inverse_two = normalize(second_sum, norm2_gain, norm2_shift, features)
    qkv_full, out_full, in_full, down_full = (
        lax.all_gather(qkv_weight, "row", axis=0, tiled=True),
        lax.all_gather(out_weight, "row", axis=0, tiled=True),
        lax.all_gather(in_weight, "row", axis=0, tiled=True),
        lax.all_gather(down_weight, "row", axis=0, tiled=True),
    )
    tokens_full, hidden_full = (
        lax.all_gather(tokens, "col", axis=1, tiled=True),
        lax.all_gather(hidden_low, "col", axis=1, tiled=True),
    )
    upstream = cotangent.astype(jnp.float32)
    gain_two_grad = jnp.sum(upstream * normal_two, 0)
    shift_two_grad = jnp.sum(upstream, 0)
    grad_second = normalize_back(upstream, normal_two, inverse_two, norm2_gain, features)
    grad_fed = grad_second.astype(jnp.bfloat16)
    down_bias_grad = jnp.sum(grad_fed.astype(jnp.float32), 0)
    fed_full = widen_grad(grad_fed)
    down_grad = jnp.einsum("to,tf->of", fed_full, activated, preferred_element_type=jnp.float32)
    act_grad = jnp.dot(fed_full, down_full, preferred_element_type=jnp.float32)
    unused_value, gelu_pull = jax.vjp(exact_gelu, pre_act)
    pre_grad = gelu_pull(act_grad)[0].astype(jnp.bfloat16)
    in_bias_grad = jnp.sum(pre_grad.astype(jnp.float32), 0)
    in_grad = jnp.einsum("td,tf->df", hidden_full, pre_grad, preferred_element_type=jnp.float32)
    hidden_grad = (
        reduce_grad(jnp.einsum("tf,df->td", pre_grad, in_full, preferred_element_type=jnp.float32))
        + grad_second
    )
    gain_one_grad = jnp.sum(hidden_grad * normal_one, 0)
    shift_one_grad = jnp.sum(hidden_grad, 0)
    grad_first = normalize_back(hidden_grad, normal_one, inverse_one, norm1_gain, features)
    grad_attended = grad_first.astype(jnp.bfloat16)
    out_bias_grad = jnp.sum(grad_attended.astype(jnp.float32), 0)
    attended_full = widen_grad(grad_attended)
    out_grad = jnp.einsum("to,tf->of", attended_full, context, preferred_element_type=jnp.float32)
    context_grad = jnp.dot(attended_full, out_full, preferred_element_type=jnp.float32).astype(
        jnp.bfloat16
    )
    context_split = context_grad.reshape(sequences, SEQ_LEN, heads_here, HEAD_DIM)
    qkv_grads = lax.map(attend_back, (queries, key_rows, values, context_split, logsums, lengths))
    qkv_grads = qkv_grads.reshape(token_count, 3, local_width)
    grad_float = qkv_grads.astype(jnp.float32)
    qv_bias_grad = jnp.stack([jnp.sum(grad_float[:, 0], 0), jnp.sum(grad_float[:, 2], 0)])
    qkv_grad = jnp.einsum("td,tsf->dsf", tokens_full, qkv_grads, preferred_element_type=jnp.float32)
    tokens_grad = (
        reduce_grad(
            jnp.einsum("tsf,dsf->td", qkv_grads, qkv_full, preferred_element_type=jnp.float32)
        )
        + grad_first
    )
    weight_grads = (
        lax.psum_scatter(
            qkv_grad.astype(jnp.bfloat16), "row", scatter_dimension=0, tiled=True
        ).astype(jnp.float32),
        lax.psum_scatter(
            out_grad.astype(jnp.bfloat16), "row", scatter_dimension=0, tiled=True
        ).astype(jnp.float32),
        lax.psum_scatter(
            in_grad.astype(jnp.bfloat16), "row", scatter_dimension=0, tiled=True
        ).astype(jnp.float32),
        lax.psum_scatter(
            down_grad.astype(jnp.bfloat16), "row", scatter_dimension=0, tiled=True
        ).astype(jnp.float32),
    )
    small_grads = lax.psum(
        (
            qv_bias_grad,
            out_bias_grad,
            gain_one_grad,
            shift_one_grad,
            in_bias_grad,
            down_bias_grad,
            gain_two_grad,
            shift_two_grad,
        ),
        "row",
    )
    return (
        output.astype(jnp.bfloat16),
        tokens_grad,
        weight_grads[0],
        small_grads[0],
        weight_grads[1],
        small_grads[1],
        small_grads[2],
        small_grads[3],
        weight_grads[2],
        small_grads[4],
        weight_grads[3],
        small_grads[5],
        small_grads[6],
        small_grads[7],
    )


def hop(array, axis, bit, size):
    return lax.ppermute(array, axis, [(place, place ^ bit) for place in range(size)])


def block_axis(bit, rows):
    return (rows // bit).bit_length() - 2


def gather_steps(shard, order, rows):
    levels = rows.bit_length() - 2
    held = shard.reshape((1,) * levels + shard.shape)
    for bit in order:
        if bit == 0:
            held = jnp.concatenate([held, hop(held, "col", 1, 2)], axis=-1)
        else:
            held = jnp.concatenate([held, hop(held, "row", bit, rows)], axis=block_axis(bit, rows))
        held = yield held
    held = held.reshape(-1, held.shape[-1])
    yield held, hop(held, "row", 1, rows)


def scatter_steps(kept, sent, order, rows):
    levels = rows.bit_length() - 2
    total = (kept + hop(sent, "row", 1, rows).astype(jnp.float32)).astype(jnp.bfloat16)
    yield total
    total = total.reshape((2,) * levels + (-1, total.shape[-1]))
    for place, bit in enumerate(order):
        axis = total.ndim - 1 if bit == 0 else block_axis(bit, rows)
        half = total.shape[axis] // 2
        mine = lax.slice_in_dim(total, 0, half, axis=axis)
        other = lax.slice_in_dim(total, half, 2 * half, axis=axis)
        arrived = hop(other, "col", 1, 2) if bit == 0 else hop(other, "row", bit, rows)
        summed = mine.astype(jnp.float32) + arrived.astype(jnp.float32)
        total = summed.astype(jnp.bfloat16)
        if place + 1 < len(order):
            yield total
    yield summed.reshape(-1, summed.shape[-1])


def last(steps):
    held = None
    for held in steps:
        pass
    return held


def finish(steps, held):
    try:
        while True:
            held = steps.send(held)
    except StopIteration:
        return held


def relative_blocks(vectors, row, rows):
    levels = rows.bit_length() - 1
    count = vectors.shape[0]
    split = vectors.reshape((count,) + (2,) * levels + (-1,))
    for level in range(levels):
        flag = (row >> (levels - 1 - level)) & 1
        split = jnp.where(flag == 1, jnp.flip(split, 1 + level), split)
    return split


def to_relative(vectors, row, rows):
    split = relative_blocks(vectors, row, rows)
    levels = rows.bit_length() - 1
    return jnp.moveaxis(split, levels, 1).reshape(vectors.shape)


def from_relative(vectors, row, rows):
    levels = rows.bit_length() - 1
    count = vectors.shape[0]
    split = vectors.reshape((count,) + (2,) * levels + (-1,))
    split = jnp.moveaxis(split, 1, levels).reshape(vectors.shape)
    return relative_blocks(split, row, rows).reshape(vectors.shape)


def order_matrix(row, col, rows, features):
    block = features // rows
    half = features // 2
    came = lax.broadcasted_iota(jnp.int32, (features, features), 0)
    came = jnp.where(came < half, came + col * half, came - half + (1 - col) * half)
    goes = lax.broadcasted_iota(jnp.int32, (features, features), 1)
    place = goes // block
    low = place // (rows // 2)
    natural = (place % (rows // 2)) * 2 + low
    goes = (natural ^ row) * block + goes % block
    return (came == goes).astype(jnp.bfloat16)


def params(limit_mib=48):
    return pltpu.CompilerParams(vmem_limit_bytes=limit_mib * 2**20)


def cost(flops, moved, transcendentals=0):
    return pl.CostEstimate(flops=flops, bytes_accessed=moved, transcendentals=transcendentals)


def run(kernel, name, grid, operands, in_specs, out_specs, out_shape, estimate, needs=(), through=(), scalars=(), fill=None):
    lead = len(scalars) + len(operands)
    extra = len(needs) + len(through)
    outs = len(out_shape)
    stay = pl.BlockSpec(memory_space=pltpu.HBM)
    aliases = {lead + len(needs) + place: outs + place for place in range(len(through))}
    for operand, out in (fill or {}).items():
        aliases[len(scalars) + operand] = out

    def body(*refs):
        kernel(*refs[:lead], *refs[lead + extra : lead + extra + outs])

    return pl.pallas_call(
        body,
        grid_spec=pltpu.PrefetchScalarGridSpec(
            num_scalar_prefetch=len(scalars),
            grid=grid,
            in_specs=list(in_specs) + [stay] * extra,
            out_specs=list(out_specs) + [stay] * len(through),
        ),
        out_shape=list(out_shape) + [jax.ShapeDtypeStruct(array.shape, array.dtype) for array in through],
        input_output_aliases=aliases,
        compiler_params=params(),
        cost_estimate=estimate,
        name=name,
    )(*scalars, *operands, *needs, *through)


def dot_nn(left, right):
    return lax.dot_general(left, right, (((1,), (0,)), ((), ())), preferred_element_type=jnp.float32)


def dot_nt(left, right):
    return lax.dot_general(left, right, (((1,), (1,)), ((), ())), preferred_element_type=jnp.float32)


def chunks(size, step):
    return [slice(start, start + step) for start in range(0, size, step)]


ROW_CHUNK = 256


def project_kernel(x_ref, first_ref, second_ref, bias_ref, out_ref):
    depth = first_ref.shape[0]
    for rows in chunks(x_ref.shape[0], ROW_CHUNK):
        total = dot_nn(x_ref[rows, :depth], first_ref[...]) + dot_nn(x_ref[rows, depth:], second_ref[...])
        out_ref[rows, :] = (total + bias_ref[...]).astype(out_ref.dtype)


def by_columns(array, tile):
    return pl.BlockSpec((array.shape[0], tile), lambda n, *_: (0, n))


def whole(array):
    return pl.BlockSpec(array.shape, lambda m, *_: (0,) * array.ndim)


def by_rows(array, tile):
    return pl.BlockSpec((tile, array.shape[1]), lambda m, *_: (m, 0))


def shaped(tokens, width, dtype):
    return jax.ShapeDtypeStruct((tokens, width), dtype)


def project(x, weight, bias, tile, needs=(), through=()):
    tokens, features = x.shape
    width = weight[0].shape[1]
    result = shaped(tokens, width, jnp.bfloat16)
    return run(
        project_kernel,
        "project",
        (width // tile,),
        (x, *weight, bias),
        [whole(x), by_columns(weight[0], tile), by_columns(weight[1], tile), by_columns(bias, tile)],
        [by_columns(result, tile)],
        [result],
        cost(2 * tokens * features * width, 2 * (tokens * features + features * width + tokens * width)),
        needs,
        through,
    )


def gelu_parts(value):
    size = jnp.abs(value) * (0.5**0.5)
    near = 1.0 / (1.0 + 0.3275911 * size)
    bell = jnp.exp(-0.5 * value * value)
    series = near * (0.127414796 + near * (-0.142248368 + near * (0.7107068705 + near * (-0.7265760135 + near * 0.5307027145))))
    tail = series * bell
    below = jnp.where(value >= 0, 1.0 - tail, tail)
    return below, value * bell * 0.3989422804014327


def widen_kernel(x_ref, first_ref, second_ref, bias_ref, active_ref, slope_ref):
    depth = first_ref.shape[0]
    for rows in chunks(x_ref.shape[0], ROW_CHUNK):
        total = dot_nn(x_ref[rows, :depth], first_ref[...]) + dot_nn(x_ref[rows, depth:], second_ref[...])
        total = total + bias_ref[...]
        below, slope = gelu_parts(total)
        active_ref[rows, :] = (total * below).astype(jnp.bfloat16)
        slope_ref[rows, :] = (below + slope).astype(jnp.bfloat16)


def feed_in(x, weight, bias, tile, needs=(), through=()):
    tokens, features = x.shape
    width = weight[0].shape[1]
    result = shaped(tokens, width, jnp.bfloat16)
    return run(
        widen_kernel,
        "feed_in",
        (width // tile,),
        (x, *weight, bias),
        [whole(x), by_columns(weight[0], tile), by_columns(weight[1], tile), by_columns(bias, tile)],
        [by_columns(result, tile)] * 2,
        [result] * 2,
        cost(4 * tokens * features * width, 2 * (tokens * features + features * width + 2 * tokens * width)),
        needs,
        through,
    )


def unfeed_kernel(x_ref, first_ref, second_ref, slope_ref, out_ref, sum_ref):
    depth = first_ref.shape[0]
    column_sum = jnp.zeros(sum_ref.shape, jnp.float32)
    for rows in chunks(x_ref.shape[0], ROW_CHUNK):
        total = dot_nn(x_ref[rows, :depth], first_ref[...]) + dot_nn(x_ref[rows, depth:], second_ref[...])
        low = (total * slope_ref[rows, :].astype(jnp.float32)).astype(jnp.bfloat16)
        out_ref[rows, :] = low
        column_sum += jnp.sum(low.astype(jnp.float32), 0, keepdims=True)
    sum_ref[...] = column_sum


def feed_back(x, weight, slope, tile, needs=()):
    tokens, features = x.shape
    width = weight[0].shape[1]
    results = [shaped(tokens, width, jnp.bfloat16), shaped(1, width, jnp.float32)]
    return run(
        unfeed_kernel,
        "feed_back",
        (width // tile,),
        (x, *weight, slope),
        [whole(x), by_columns(weight[0], tile), by_columns(weight[1], tile), by_columns(slope, tile)],
        [by_columns(result, tile) for result in results],
        results,
        cost(2 * tokens * features * width, 2 * (tokens * features + features * width + 2 * tokens * width)),
        needs,
    )


def both_halves(x, first_ref, second_ref):
    return jnp.concatenate([dot_nt(x, first_ref[...]), dot_nt(x, second_ref[...])], 1)


def layer_norm_rows(summed):
    center = jnp.mean(summed, 1, keepdims=True)
    shifted = summed - center
    inverse = lax.rsqrt(jnp.mean(shifted * shifted, 1, keepdims=True) + epsilon)
    return shifted * inverse, inverse


def layer_norm_back(gradient, normal, inverse, gain):
    scaled = gradient * gain
    first = jnp.mean(scaled, 1, keepdims=True)
    second = jnp.mean(scaled * normal, 1, keepdims=True)
    return inverse * (scaled - first - normal * second)


def attended_kernel(context_ref, first_ref, second_ref, x_ref, vector_ref, normal_ref, low_ref, inverse_ref):
    attended = both_halves(context_ref[...], first_ref, second_ref) + vector_ref[0:1, :]
    normal, inverse = layer_norm_rows(x_ref[...].astype(jnp.float32) + attended)
    normal_ref[...] = normal
    low_ref[...] = (normal * vector_ref[1:2, :] + vector_ref[2:3, :]).astype(jnp.bfloat16)
    inverse_ref[...] = jnp.broadcast_to(inverse, inverse_ref.shape)


def attended_norm(context, weight, x, vectors, tile, needs=(), through=()):
    tokens, features = x.shape
    results = [
        shaped(tokens, features, jnp.float32),
        shaped(tokens, features, jnp.bfloat16),
        shaped(tokens, 128, jnp.float32),
    ]
    return run(
        attended_kernel,
        "attended_norm",
        (tokens // tile,),
        (context, *weight, x, vectors),
        [by_rows(context, tile), whole(weight[0]), whole(weight[1]), by_rows(x, tile), whole(vectors)],
        [by_rows(result, tile) for result in results],
        results,
        cost(2 * tokens * features * context.shape[1], 14 * tokens * features),
        needs,
        through,
    )


def fed_kernel(
    near_ref, far_ref, near0_ref, near1_ref, far0_ref, far1_ref, normal_ref, cotangent_ref, vector_ref, order_ref,
    out_ref, grad_ref, low_ref, sum_ref,
):
    fed = both_halves(near_ref[...], near0_ref, near1_ref) + both_halves(far_ref[...], far0_ref, far1_ref)
    fed = fed + vector_ref[3:4, :]
    hidden = normal_ref[...] * vector_ref[1:2, :] + vector_ref[2:3, :]
    normal, inverse = layer_norm_rows(hidden + fed)
    output = (normal * vector_ref[4:5, :] + vector_ref[5:6, :]).astype(jnp.bfloat16)
    out_ref[...] = dot_nt(output, order_ref[...]).astype(jnp.bfloat16)
    upstream = cotangent_ref[...].astype(jnp.float32)
    gradient = layer_norm_back(upstream, normal, inverse, vector_ref[4:5, :])
    grad_ref[...] = gradient
    low = gradient.astype(jnp.bfloat16)
    low_ref[...] = low

    @pl.when(pl.program_id(0) == 0)
    def clear():
        sum_ref[...] = jnp.zeros_like(sum_ref)

    sum_ref[0:1, :] += jnp.sum(upstream * normal, 0, keepdims=True)
    sum_ref[1:2, :] += jnp.sum(upstream, 0, keepdims=True)
    sum_ref[2:3, :] += jnp.sum(low.astype(jnp.float32), 0, keepdims=True)


def fed_norm(actives, weights, normal, cotangent, vectors, order, tile):
    tokens, features = normal.shape
    halves = [half for weight in weights for half in weight]
    results = [
        shaped(tokens, features, jnp.bfloat16),
        shaped(tokens, features, jnp.float32),
        shaped(tokens, features, jnp.bfloat16),
    ]
    sums = shaped(8, features, jnp.float32)
    units = 2 * actives[0].shape[1]
    return run(
        fed_kernel,
        "fed_norm",
        (tokens // tile,),
        (*actives, *halves, normal, cotangent, vectors, order),
        [by_rows(active, tile) for active in actives]
        + [whole(half) for half in halves]
        + [by_rows(normal, tile), by_rows(cotangent, tile), whole(vectors), whole(order)],
        [by_rows(result, tile) for result in results] + [whole(sums)],
        results + [sums],
        cost(2 * tokens * features * (units + features), 2 * units * (tokens + features) + 14 * tokens * features),
    )


def hidden_kernel(
    near_ref, far_ref, near0_ref, near1_ref, far0_ref, far1_ref, second_grad_ref, normal_ref, inverse_ref, vector_ref,
    grad_ref, low_ref, sum_ref,
):
    gradient = both_halves(near_ref[...], near0_ref, near1_ref) + both_halves(far_ref[...], far0_ref, far1_ref)
    gradient = gradient + second_grad_ref[...]
    normal = normal_ref[...]
    first = layer_norm_back(gradient, normal, inverse_ref[:, 0:1], vector_ref[1:2, :])
    grad_ref[...] = first
    low = first.astype(jnp.bfloat16)
    low_ref[...] = low

    @pl.when(pl.program_id(0) == 0)
    def clear():
        sum_ref[...] = jnp.zeros_like(sum_ref)

    sum_ref[0:1, :] += jnp.sum(gradient * normal, 0, keepdims=True)
    sum_ref[1:2, :] += jnp.sum(gradient, 0, keepdims=True)
    sum_ref[2:3, :] += jnp.sum(low.astype(jnp.float32), 0, keepdims=True)


def hidden_back(pre_grads, weights, second_grad, normal, inverse, vectors, tile, needs=()):
    tokens, features = normal.shape
    halves = [half for weight in weights for half in weight]
    results = [shaped(tokens, features, jnp.float32), shaped(tokens, features, jnp.bfloat16)]
    sums = shaped(8, features, jnp.float32)
    units = 2 * pre_grads[0].shape[1]
    return run(
        hidden_kernel,
        "hidden_back",
        (tokens // tile,),
        (*pre_grads, *halves, second_grad, normal, inverse, vectors),
        [by_rows(pre_grad, tile) for pre_grad in pre_grads]
        + [whole(half) for half in halves]
        + [by_rows(second_grad, tile), by_rows(normal, tile), by_rows(inverse, tile), whole(vectors)],
        [by_rows(result, tile) for result in results] + [whole(sums)],
        results + [sums],
        cost(2 * tokens * features * units, 2 * units * (tokens + features) + 14 * tokens * features),
        needs,
    )


def tokens_kernel(dq_ref, dk_ref, dv_ref, q0_ref, q1_ref, k0_ref, k1_ref, v0_ref, v1_ref, first_ref, order_ref, out_ref):
    total = (
        both_halves(dq_ref[...], q0_ref, q1_ref)
        + both_halves(dk_ref[...], k0_ref, k1_ref)
        + both_halves(dv_ref[...], v0_ref, v1_ref)
        + first_ref[...]
    )
    out_ref[...] = dot_nt(total.astype(jnp.bfloat16), order_ref[...]).astype(jnp.bfloat16)


def tokens_back(grads, weights, first_grad, order, tile, needs=()):
    tokens, features = first_grad.shape
    halves = [half for weight in weights for half in weight]
    result = shaped(tokens, features, jnp.bfloat16)
    return run(
        tokens_kernel,
        "tokens_back",
        (tokens // tile,),
        (*grads, *halves, first_grad, order),
        [by_rows(grad, tile) for grad in grads]
        + [whole(half) for half in halves]
        + [by_rows(first_grad, tile), whole(order)],
        [by_rows(result, tile)],
        [result],
        cost(8 * tokens * features * features, 20 * tokens * features),
        needs,
    )


def key_bias(length, keys):
    place = lax.broadcasted_iota(jnp.int32, (keys, 1), 0)
    return jnp.where(place < length, 0.0, masked_score)


def attend_kernel(length_ref, q_ref, k_ref, v_ref, context_ref, logsum_ref):
    bias = key_bias(length_ref[pl.program_id(0)], k_ref.shape[0])
    queries = q_ref[...] * (HEAD_DIM**-0.5)
    key_rows = k_ref[...]
    values = v_ref[...].T
    lane = lax.broadcasted_iota(jnp.int32, queries.shape, 1) // HEAD_DIM
    parts = []
    for head in range(queries.shape[1] // HEAD_DIM):
        one = jnp.where(lane == head, queries, jnp.zeros_like(queries))
        scores = dot_nt(key_rows, one) + bias
        top = jnp.max(scores, 0, keepdims=True)
        raised = jnp.exp(scores - top)
        total = jnp.sum(raised, 0, keepdims=True)
        logsum_ref[0, head : head + 1, :] = top + jnp.log(total)
        mixed = dot_nn(values[head * HEAD_DIM : (head + 1) * HEAD_DIM, :], raised.astype(jnp.bfloat16))
        parts.append(mixed / total)
    context_ref[...] = jnp.concatenate(parts, 0).T.astype(jnp.bfloat16)


def attend(queries, key_rows, values, lengths, needs=(), through=()):
    tokens, features = queries.shape
    sequences = lengths.shape[0]
    wide = 2 * HEAD_DIM
    spec = pl.BlockSpec((SEQ_LEN, wide), lambda s, h, _: (s, h))
    steps = features // wide
    return run(
        attend_kernel,
        "attend",
        (sequences, steps),
        (queries, key_rows, values),
        [spec] * 3,
        [spec, pl.BlockSpec((1, 8, SEQ_LEN), lambda s, h, _: (s * steps + h, 0, 0))],
        [shaped(tokens, features, jnp.bfloat16), jax.ShapeDtypeStruct((sequences * steps, 8, SEQ_LEN), jnp.float32)],
        cost(16 * tokens * features * SEQ_LEN, 8 * tokens * features),
        needs,
        through,
        (lengths,),
    )


def attend_back_kernel(length_ref, q_ref, k_ref, v_ref, grad_ref, logsum_ref, dq_ref, dk_ref, dv_ref, sum_ref):
    bias = key_bias(length_ref[pl.program_id(0)], k_ref.shape[0])
    queries = q_ref[...] * (HEAD_DIM**-0.5)
    key_rows = k_ref[...]
    key_columns = key_rows.T
    values = v_ref[...]
    grads = grad_ref[...]
    lane = lax.broadcasted_iota(jnp.int32, queries.shape, 1) // HEAD_DIM
    query_parts = []
    key_grad = jnp.zeros(queries.shape, jnp.float32)
    value_grad = jnp.zeros(queries.shape, jnp.float32)
    for head in range(queries.shape[1] // HEAD_DIM):
        one = jnp.where(lane == head, queries, jnp.zeros_like(queries))
        one_grad = jnp.where(lane == head, grads, jnp.zeros_like(grads))
        chances = jnp.exp(dot_nt(key_rows, one) + bias - logsum_ref[0, head : head + 1, :])
        chance_grad = dot_nt(values, one_grad)
        value_grad += dot_nn(chances.astype(jnp.bfloat16), one_grad)
        inner = jnp.sum(chances * chance_grad, 0, keepdims=True)
        score_grad = (chances * (chance_grad - inner)).astype(jnp.bfloat16)
        key_grad += dot_nn(score_grad, one)
        query_parts.append(dot_nn(key_columns[head * HEAD_DIM : (head + 1) * HEAD_DIM, :], score_grad))
    query_grad = jnp.concatenate(query_parts, 0) * (HEAD_DIM**-0.5)
    query_grad = query_grad.T.astype(jnp.bfloat16)
    value_grad = value_grad.astype(jnp.bfloat16)
    dq_ref[...] = query_grad
    dk_ref[...] = key_grad.astype(jnp.bfloat16)
    dv_ref[...] = value_grad
    sum_ref[...] = jnp.zeros_like(sum_ref)
    sum_ref[0, 0:1, :] = jnp.sum(query_grad.astype(jnp.float32), 0, keepdims=True)
    sum_ref[0, 1:2, :] = jnp.sum(value_grad.astype(jnp.float32), 0, keepdims=True)


def attend_grads(queries, key_rows, values, context_grad, logsums, lengths, part, filled=(), needs=()):
    tokens, features = queries.shape
    sequences = lengths.shape[0]
    wide = 2 * HEAD_DIM
    steps = features // wide
    count = steps // 2
    first = part * count
    spec = pl.BlockSpec((SEQ_LEN, wide), lambda s, h, _: (s, first + h))
    sums_spec = pl.BlockSpec((1, 8, wide), lambda s, h, _: (s, 0, first + h))
    results = [shaped(tokens, features, jnp.bfloat16)] * 3
    results = results + [jax.ShapeDtypeStruct((sequences, 8, features), jnp.float32)]

    def kernel(*refs):
        attend_back_kernel(*refs[:6], *refs[6 + len(filled) :])

    return run(
        kernel,
        "attend_grads",
        (sequences, count),
        (queries, key_rows, values, context_grad, logsums, *filled),
        [spec] * 4
        + [pl.BlockSpec((1, 8, SEQ_LEN), lambda s, h, _: (s * steps + first + h, 0, 0))]
        + [pl.BlockSpec(memory_space=pltpu.HBM)] * len(filled),
        [spec] * 3 + [sums_spec],
        results,
        cost(20 * tokens * features * SEQ_LEN, 7 * tokens * features),
        needs,
        (),
        (lengths,),
        {5 + place: place for place in range(len(filled))},
    )


def weight_grad(left, right):
    half = left.shape[1] // 2

    def part(columns):
        return lax.dot_general(left[:, columns], right, (((0,), (0,)), ((), ())), preferred_element_type=jnp.float32)

    return part(slice(0, half)), part(slice(half, 2 * half)).astype(jnp.bfloat16)


def by_tokens(
    tokens,
    qkv_weight,
    qv_bias,
    out_weight,
    out_bias,
    norm1_gain,
    norm1_shift,
    in_weight,
    in_bias,
    down_weight,
    down_bias,
    norm2_gain,
    norm2_shift,
    lengths,
    cotangent,
):
    rows = lax.axis_size("row")
    row, col = lax.axis_index("row"), lax.axis_index("col")
    local_width = tokens.shape[1]
    features = 2 * local_width
    share = tokens.shape[0] // 2
    bits = [1 << level for level in range(1, rows.bit_length() - 1)]
    cross, line = bits[0], bits[:0:-1]
    via_col = line + [cross, 0]
    via_row = line + [0, cross]
    via_line = [cross, 0] + line

    def take(array):
        mine = lax.dynamic_slice_in_dim(array, col * share, share, 0)
        other = lax.dynamic_slice_in_dim(array, (1 - col) * share, share, 0)
        return jnp.concatenate([mine, hop(other, "col", 1, 2)], 1)

    def give(array):
        mine, arrived = array[:, :local_width], hop(array[:, local_width:], "col", 1, 2)
        return jnp.where(col == 0, jnp.concatenate([mine, arrived], 0), jnp.concatenate([arrived, mine], 0))

    def gathering(shard, order):
        return gather_steps(shard, order, rows)

    def gathered(shard, order):
        steps = gathering(shard, order)
        return finish(steps, next(steps))

    def advance(steps, count):
        held = next(steps)
        for _ in range(count - 1):
            held = steps.send(held)
        return held

    levels = len(line)
    units = in_weight.shape[1] // 2
    order = order_matrix(row, col, rows, features)
    x = dot_nn(take(tokens), order).astype(jnp.bfloat16)
    query_weight = gathered(qkv_weight[:, 0], via_col)
    key_weight = gathered(qkv_weight[:, 1], via_row)
    value_weight = gathered(qkv_weight[:, 2], via_line)
    out_full = gathered(out_weight, via_line)
    in_steps = [gathering(in_weight[:, :units], via_col), gathering(in_weight[:, units:], via_row)]
    down_steps = [gathering(down_weight[:, :units], via_col), gathering(down_weight[:, units:], via_row)]
    in_held = [advance(steps, levels) for steps in in_steps]
    down_held = [advance(steps, levels) for steps in down_steps]

    small = jnp.stack([out_bias, norm1_gain, norm1_shift, down_bias, norm2_gain, norm2_shift, qv_bias[0], qv_bias[1]])
    small = jnp.concatenate([small, in_bias.reshape(-1, local_width)], 0)
    far = hop(small, "col", 1, 2)
    pair = jnp.concatenate([small, far], 1)
    straight = jnp.where(col == 0, pair[:6], jnp.concatenate([far[:6], small[:6]], 1))
    vectors = jnp.pad(to_relative(straight, row, rows), ((0, 2), (0, 0)))
    in_biases = [
        jnp.concatenate([one.reshape(2, 1, -1)[half] for one in (small[8:], far[8:])], 1) for half in range(2)
    ]
    own_lengths = lax.dynamic_slice_in_dim(lengths, col * (lengths.shape[0] // 2), lengths.shape[0] // 2)

    (values,) = project(x, value_weight, pair[7:8], 512)
    (key_rows,) = project(x, key_weight, jnp.zeros((1, features), jnp.float32), 512)
    queries, *in_held = project(x, query_weight, pair[6:7], 512, through=in_held)
    in_held = [steps.send(held) for steps, held in zip(in_steps, in_held)]
    context, logsums, *down_held = attend(queries, key_rows, values, own_lengths, through=down_held)
    down_held = [steps.send(held) for steps, held in zip(down_steps, down_held)]
    cotangent_far = lax.dynamic_slice_in_dim(cotangent, (1 - col) * share, share, 0)
    normal_one, hidden_low, inverse_one, *down_held, cotangent_far = attended_norm(
        context, out_full, x, vectors, 256, needs=in_held, through=[*down_held, cotangent_far]
    )
    in_full = [finish(steps, held) for steps, held in zip(in_steps, in_held)]
    active_near, slope_near = feed_in(hidden_low, in_full[0], in_biases[0], 512)
    active_far, slope_far = feed_in(hidden_low, in_full[1], in_biases[1], 512)
    down_full = [finish(steps, held) for steps, held in zip(down_steps, down_held)]
    cotangent_near = lax.dynamic_slice_in_dim(cotangent, col * share, share, 0)
    upstream = jnp.concatenate([cotangent_near, hop(cotangent_far, "col", 1, 2)], 1)
    upstream = dot_nn(upstream, order).astype(jnp.bfloat16)
    output, grad_second, grad_fed, sums_two = fed_norm(
        (active_near, active_far), down_full, normal_one, upstream, vectors, order, 256
    )

    back = line[::-1]
    orders = ([cross, 0] + back, [0, cross] + back)
    down_parts = [weight_grad(grad_fed, active) for active in (active_near, active_far)]
    pre_near, sum_near = feed_back(grad_fed, down_full[0], slope_near, 512, [sent for _, sent in down_parts])
    pre_far, sum_far = feed_back(grad_fed, down_full[1], slope_far, 512)
    down_steps = [scatter_steps(*parts, order_of, rows) for parts, order_of in zip(down_parts, orders)]
    down_held = [next(steps) for steps in down_steps]
    in_parts = [weight_grad(hidden_low, pre_grad) for pre_grad in (pre_near, pre_far)]
    grad_first, grad_attended, sums_one = hidden_back(
        (pre_near, pre_far), in_full, grad_second, normal_one, inverse_one, vectors, 256,
        [*down_held, *[sent for _, sent in in_parts]],
    )
    in_steps = [scatter_steps(*parts, order_of, rows) for parts, order_of in zip(in_parts, orders)]
    in_held = [next(steps) for steps in in_steps]
    out_parts = weight_grad(grad_attended, context)
    (context_grad,) = project(
        grad_attended, out_full, jnp.zeros((1, features), jnp.float32), 512, [*in_held, out_parts[1]]
    )
    out_steps = scatter_steps(*out_parts, back + [cross, 0], rows)
    out_held = next(out_steps)
    attention = (queries, key_rows, values, context_grad, logsums, own_lengths)
    grads = attend_grads(*attention, 1, (), [out_held])
    down_held = [next(steps) for steps in down_steps]
    out_held = next(out_steps)
    dq, dk, dv, qv_sums = attend_grads(*attention, 0, grads, [*down_held, out_held])
    query_parts, key_parts, value_parts = weight_grad(x, dq), weight_grad(x, dk), weight_grad(x, dv)
    in_held = [next(steps) for steps in in_steps]
    down_held = [next(steps) for steps in down_steps]
    (tokens_grad,) = tokens_back(
        (dq, dk, dv), (query_weight, key_weight, value_weight), grad_first, order, 256,
        [query_parts[1], key_parts[1], value_parts[1], *in_held, *down_held],
    )
    query_grad = last(scatter_steps(*query_parts, orders[1], rows))
    key_grad = last(scatter_steps(*key_parts, orders[0], rows))
    value_grad = last(scatter_steps(*value_parts, back + [cross, 0], rows))
    out_grad = last(out_steps)
    in_grad = jnp.concatenate([last(steps) for steps in in_steps], 1)
    down_grad = jnp.concatenate([last(steps) for steps in down_steps], 1)

    def straighten(array):
        split = array.reshape(array.shape[0], 2, -1)
        return jnp.where(col == 0, split, jnp.flip(split, 1)).reshape(array.shape[0], -1)

    def own(array):
        return lax.dynamic_slice_in_dim(array, col * (array.shape[1] // 2), array.shape[1] // 2, 1)

    feature_sums = from_relative(jnp.concatenate([sums_two[:3], sums_one[:3]], 0), row, rows)
    unit_sums = straighten(jnp.concatenate([sum_near, sum_far], 0))
    qv_sums = straighten(jnp.sum(qv_sums, 0)[:2])
    sums = jnp.concatenate([feature_sums, unit_sums.reshape(-1, features), qv_sums], 0)
    sums = sums + hop(sums, "col", 1, 2)
    for bit in [1, *bits]:
        sums = sums + hop(sums, "row", bit, rows)
    feature_sums = own(sums[:6])
    in_bias_grad = own(sums[6:-2].reshape(2, -1)).reshape(-1)
    return (
        give(output),
        give(tokens_grad).astype(jnp.float32),
        jnp.stack([query_grad, key_grad, value_grad], 1),
        own(sums[-2:]),
        out_grad,
        feature_sums[5],
        feature_sums[3],
        feature_sums[4],
        in_grad,
        in_bias_grad,
        down_grad,
        feature_sums[2],
        feature_sums[0],
        feature_sums[1],
    )


def device_program(*arrays):
    rows, cols = lax.axis_size("row"), lax.axis_size("col")
    sequences = arrays[13].shape[0]
    if cols == 2 and rows >= 8 and rows & (rows - 1) == 0 and sequences % 2 == 0:
        return by_tokens(*arrays)
    return on_device(*arrays)


def solution(mesh):
    placed = (
        P("row", "col"),
        P("row", None, "col"),
        P(None, "col"),
        P("row", "col"),
        P("col"),
        P("col"),
        P("col"),
        P("row", "col"),
        P("col"),
        P("row", "col"),
        P("col"),
        P("col"),
        P("col"),
        P("row"),
        P("row", "col"),
    )
    return jax.shard_map(
        device_program,
        mesh=mesh,
        in_specs=placed,
        out_specs=(
            P("row", "col"),
            P("row", "col"),
            P("row", None, "col"),
            P(None, "col"),
            P("row", "col"),
            P("col"),
            P("col"),
            P("col"),
            P("row", "col"),
            P("col"),
            P("row", "col"),
            P("col"),
            P("col"),
            P("col"),
        ),
        check_vma=False,
    )
```

```python
import jax
import jax.numpy as jnp
from jax import lax
from jax.experimental import pallas as pl
from jax.experimental.pallas import tpu as pltpu
from jax.sharding import PartitionSpec as P

HEAD_DIM = 64
SEQ_LEN = 512


epsilon = 1e-05
masked_score = -1000000000.0


def widen(portion):
    return lax.all_gather(portion, "col", axis=1, tiled=True)


def widen_grad(portion):
    return lax.all_gather(portion, "col", axis=1, tiled=True)


def reduce_out(partial_rows):
    return lax.psum_scatter(partial_rows, "col", scatter_dimension=1, tiled=True)


def reduce_grad(partial_rows):
    return lax.psum_scatter(partial_rows, "col", scatter_dimension=1, tiled=True)


def exact_gelu(values):
    return jax.nn.gelu(values, approximate=False)


def normalize(summed, norm_gain, norm_shift, features):
    moments = lax.psum((jnp.sum(summed, 1), jnp.sum(summed * summed, 1)), "col")
    center = moments[0] / features
    inverse = lax.rsqrt(moments[1] / features - center * center + epsilon)
    normal = (summed - center[:, None]) * inverse[:, None]
    return (normal * norm_gain + norm_shift, normal, inverse)


def normalize_back(gradient, normal, inverse, norm_gain, features):
    scaled = gradient * norm_gain
    moments = lax.psum((jnp.sum(scaled, 1), jnp.sum(scaled * normal, 1)), "col")
    return inverse[:, None] * (
        scaled - moments[0][:, None] / features - normal * moments[1][:, None] / features
    )


def masked_scores(queries, key_rows, length):
    factor = HEAD_DIM ** (-0.5)
    scores = (
        jnp.einsum("qhd,khd->hqk", queries, key_rows, preferred_element_type=jnp.float32) * factor
    )
    usable = jnp.arange(scores.shape[2]) < length
    return jnp.where(usable[None, None, :], scores, masked_score)


def attend_forward(element):
    queries, key_rows, values, length = element
    scores = masked_scores(queries, key_rows, length)
    highest = jnp.max(scores, 2, keepdims=True)
    raised = jnp.exp(scores - highest)
    row_total = jnp.sum(raised, 2, keepdims=True)
    chances = (raised / row_total).astype(jnp.bfloat16)
    context = jnp.einsum("hqk,khd->qhd", chances, values, preferred_element_type=jnp.float32)
    return (context.astype(jnp.bfloat16), (highest + jnp.log(row_total))[:, :, 0])


def attend_back(element):
    queries, key_rows, values, context_grad, logsum, length = element
    factor = HEAD_DIM ** (-0.5)
    scores = masked_scores(queries, key_rows, length)
    chances = jnp.exp(scores - logsum[:, :, None])
    chance_grad = jnp.einsum(
        "qhd,khd->hqk", context_grad, values, preferred_element_type=jnp.float32
    )
    value_grad = jnp.einsum(
        "hqk,qhd->khd",
        chances.astype(jnp.bfloat16),
        context_grad,
        preferred_element_type=jnp.float32,
    )
    inner = jnp.sum(chances * chance_grad, 2, keepdims=True)
    score_grad = (chances * (chance_grad - inner)).astype(jnp.bfloat16)
    query_grad = (
        jnp.einsum("hqk,khd->qhd", score_grad, key_rows, preferred_element_type=jnp.float32)
        * factor
    )
    key_grad = (
        jnp.einsum("hqk,qhd->khd", score_grad, queries, preferred_element_type=jnp.float32) * factor
    )
    return jnp.stack([query_grad, key_grad, value_grad], 1).astype(jnp.bfloat16)


def on_device(
    tokens,
    qkv_weight,
    qv_bias,
    out_weight,
    out_bias,
    norm1_gain,
    norm1_shift,
    in_weight,
    in_bias,
    down_weight,
    down_bias,
    norm2_gain,
    norm2_shift,
    lengths,
    cotangent,
):
    local_width = tokens.shape[1]
    features = local_width * lax.axis_size("col")
    token_count = tokens.shape[0]
    sequences = lengths.shape[0]
    heads_here = local_width // HEAD_DIM
    qkv_full, out_full, in_full, down_full = (
        lax.all_gather(qkv_weight, "row", axis=0, tiled=True),
        lax.all_gather(out_weight, "row", axis=0, tiled=True),
        lax.all_gather(in_weight, "row", axis=0, tiled=True),
        lax.all_gather(down_weight, "row", axis=0, tiled=True),
    )
    tokens_full = widen(tokens)
    projected = jnp.einsum("td,dsf->tsf", tokens_full, qkv_full, preferred_element_type=jnp.float32)
    qkv_bias = jnp.stack([qv_bias[0], jnp.zeros_like(qv_bias[0]), qv_bias[1]])
    qkv_rows = (projected + qkv_bias).astype(jnp.bfloat16)
    split_rows = qkv_rows.reshape(sequences, SEQ_LEN, 3, heads_here, HEAD_DIM)
    queries = split_rows[:, :, 0]
    key_rows = split_rows[:, :, 1]
    values = split_rows[:, :, 2]
    context, logsums = lax.map(attend_forward, (queries, key_rows, values, lengths))
    context = context.reshape(token_count, local_width)
    attended = (
        reduce_out(jnp.einsum("tf,of->to", context, out_full, preferred_element_type=jnp.float32))
        + out_bias
    )
    first_sum = tokens.astype(jnp.float32) + attended
    hidden_one, normal_one, inverse_one = normalize(first_sum, norm1_gain, norm1_shift, features)
    hidden_low = hidden_one.astype(jnp.bfloat16)
    hidden_full = widen(hidden_low)
    pre_act = jnp.dot(hidden_full, in_full, preferred_element_type=jnp.float32) + in_bias
    activated = exact_gelu(pre_act).astype(jnp.bfloat16)
    fed = (
        reduce_out(
            jnp.einsum("tf,of->to", activated, down_full, preferred_element_type=jnp.float32)
        )
        + down_bias
    )
    second_sum = hidden_one + fed
    output, normal_two, inverse_two = normalize(second_sum, norm2_gain, norm2_shift, features)
    qkv_full, out_full, in_full, down_full = (
        lax.all_gather(qkv_weight, "row", axis=0, tiled=True),
        lax.all_gather(out_weight, "row", axis=0, tiled=True),
        lax.all_gather(in_weight, "row", axis=0, tiled=True),
        lax.all_gather(down_weight, "row", axis=0, tiled=True),
    )
    tokens_full, hidden_full = (
        lax.all_gather(tokens, "col", axis=1, tiled=True),
        lax.all_gather(hidden_low, "col", axis=1, tiled=True),
    )
    upstream = cotangent.astype(jnp.float32)
    gain_two_grad = jnp.sum(upstream * normal_two, 0)
    shift_two_grad = jnp.sum(upstream, 0)
    grad_second = normalize_back(upstream, normal_two, inverse_two, norm2_gain, features)
    grad_fed = grad_second.astype(jnp.bfloat16)
    down_bias_grad = jnp.sum(grad_fed.astype(jnp.float32), 0)
    fed_full = widen_grad(grad_fed)
    down_grad = jnp.einsum("to,tf->of", fed_full, activated, preferred_element_type=jnp.float32)
    act_grad = jnp.dot(fed_full, down_full, preferred_element_type=jnp.float32)
    unused_value, gelu_pull = jax.vjp(exact_gelu, pre_act)
    pre_grad = gelu_pull(act_grad)[0].astype(jnp.bfloat16)
    in_bias_grad = jnp.sum(pre_grad.astype(jnp.float32), 0)
    in_grad = jnp.einsum("td,tf->df", hidden_full, pre_grad, preferred_element_type=jnp.float32)
    hidden_grad = (
        reduce_grad(jnp.einsum("tf,df->td", pre_grad, in_full, preferred_element_type=jnp.float32))
        + grad_second
    )
    gain_one_grad = jnp.sum(hidden_grad * normal_one, 0)
    shift_one_grad = jnp.sum(hidden_grad, 0)
    grad_first = normalize_back(hidden_grad, normal_one, inverse_one, norm1_gain, features)
    grad_attended = grad_first.astype(jnp.bfloat16)
    out_bias_grad = jnp.sum(grad_attended.astype(jnp.float32), 0)
    attended_full = widen_grad(grad_attended)
    out_grad = jnp.einsum("to,tf->of", attended_full, context, preferred_element_type=jnp.float32)
    context_grad = jnp.dot(attended_full, out_full, preferred_element_type=jnp.float32).astype(
        jnp.bfloat16
    )
    context_split = context_grad.reshape(sequences, SEQ_LEN, heads_here, HEAD_DIM)
    qkv_grads = lax.map(attend_back, (queries, key_rows, values, context_split, logsums, lengths))
    qkv_grads = qkv_grads.reshape(token_count, 3, local_width)
    grad_float = qkv_grads.astype(jnp.float32)
    qv_bias_grad = jnp.stack([jnp.sum(grad_float[:, 0], 0), jnp.sum(grad_float[:, 2], 0)])
    qkv_grad = jnp.einsum("td,tsf->dsf", tokens_full, qkv_grads, preferred_element_type=jnp.float32)
    tokens_grad = (
        reduce_grad(
            jnp.einsum("tsf,dsf->td", qkv_grads, qkv_full, preferred_element_type=jnp.float32)
        )
        + grad_first
    )
    weight_grads = (
        lax.psum_scatter(
            qkv_grad.astype(jnp.bfloat16), "row", scatter_dimension=0, tiled=True
        ).astype(jnp.float32),
        lax.psum_scatter(
            out_grad.astype(jnp.bfloat16), "row", scatter_dimension=0, tiled=True
        ).astype(jnp.float32),
        lax.psum_scatter(
            in_grad.astype(jnp.bfloat16), "row", scatter_dimension=0, tiled=True
        ).astype(jnp.float32),
        lax.psum_scatter(
            down_grad.astype(jnp.bfloat16), "row", scatter_dimension=0, tiled=True
        ).astype(jnp.float32),
    )
    small_grads = lax.psum(
        (
            qv_bias_grad,
            out_bias_grad,
            gain_one_grad,
            shift_one_grad,
            in_bias_grad,
            down_bias_grad,
            gain_two_grad,
            shift_two_grad,
        ),
        "row",
    )
    return (
        output.astype(jnp.bfloat16),
        tokens_grad,
        weight_grads[0],
        small_grads[0],
        weight_grads[1],
        small_grads[1],
        small_grads[2],
        small_grads[3],
        weight_grads[2],
        small_grads[4],
        weight_grads[3],
        small_grads[5],
        small_grads[6],
        small_grads[7],
    )


def hop(array, axis, bit, size):
    return lax.ppermute(array, axis, [(place, place ^ bit) for place in range(size)])


def block_axis(bit, rows):
    return (rows // bit).bit_length() - 2


class Gather:
    def __init__(self, shard, order, rows):
        self.order, self.rows = list(order), rows
        self.held = shard.reshape((1,) * (rows.bit_length() - 2) + shard.shape)
        self.flight = None

    def start(self):
        if not self.order:
            self.held = self.held.reshape(-1, self.held.shape[-1])
            self.flight = hop(self.held, "row", 1, self.rows)
        elif self.order[0] == 0:
            self.flight = hop(self.held, "col", 1, 2)
        else:
            self.flight = hop(self.held, "row", self.order[0], self.rows)

    def land(self):
        bit = self.order.pop(0)
        axis = -1 if bit == 0 else block_axis(bit, self.rows)
        self.held = jnp.concatenate([self.held, self.flight], axis=axis)

    def both(self):
        return self.held, self.flight


class Scatter:
    def __init__(self, parts, order, rows):
        self.order, self.rows = [1, *order], rows
        self.mine, other = parts
        self.flight = hop(other, "row", 1, rows)

    def land(self):
        levels = self.rows.bit_length() - 2
        self.order.pop(0)
        self.total = self.mine + self.flight.astype(jnp.float32)
        self.held = self.total.astype(jnp.bfloat16)
        if self.held.ndim == 2:
            self.held = self.held.reshape((2,) * levels + (-1, self.held.shape[-1]))

    def start(self):
        if not self.order:
            return
        bit = self.order[0]
        axis = self.held.ndim - 1 if bit == 0 else block_axis(bit, self.rows)
        half = self.held.shape[axis] // 2
        self.mine = lax.slice_in_dim(self.held, 0, half, axis=axis).astype(jnp.float32)
        other = lax.slice_in_dim(self.held, half, 2 * half, axis=axis)
        self.flight = hop(other, "col", 1, 2) if bit == 0 else hop(other, "row", bit, self.rows)

    def result(self):
        return self.total.reshape(-1, self.total.shape[-1])


def tie(value, chains, name):
    tied = lax.optimization_barrier((value, *[getattr(chain, name) for chain in chains]))
    for chain, array in zip(chains, tied[1:]):
        setattr(chain, name, array)
    return tied[0]


def point(value, land=(), start=()):
    land = [chain for chain in land if chain.order]
    if land:
        value = tie(value, land, "flight")
        for chain in land:
            chain.land()
    if start:
        value = tie(value, start, "held")
        for chain in start:
            chain.start()
    return value


def relative_blocks(vectors, row, rows):
    levels = rows.bit_length() - 1
    count = vectors.shape[0]
    split = vectors.reshape((count,) + (2,) * levels + (-1,))
    for level in range(levels):
        flag = (row >> (levels - 1 - level)) & 1
        split = jnp.where(flag == 1, jnp.flip(split, 1 + level), split)
    return split


def to_relative(vectors, row, rows):
    split = relative_blocks(vectors, row, rows)
    levels = rows.bit_length() - 1
    return jnp.moveaxis(split, levels, 1).reshape(vectors.shape)


def from_relative(vectors, row, rows):
    levels = rows.bit_length() - 1
    count = vectors.shape[0]
    split = vectors.reshape((count,) + (2,) * levels + (-1,))
    split = jnp.moveaxis(split, 1, levels).reshape(vectors.shape)
    return relative_blocks(split, row, rows).reshape(vectors.shape)


def order_matrix(row, col, rows, features):
    block = features // rows
    half = features // 2
    came = lax.broadcasted_iota(jnp.int32, (features, features), 0)
    came = jnp.where(came < half, came + col * half, came - half + (1 - col) * half)
    goes = lax.broadcasted_iota(jnp.int32, (features, features), 1)
    place = goes // block
    low = place // (rows // 2)
    natural = (place % (rows // 2)) * 2 + low
    goes = (natural ^ row) * block + goes % block
    return (came == goes).astype(jnp.bfloat16)


def params(limit_mib=48):
    return pltpu.CompilerParams(vmem_limit_bytes=limit_mib * 2**20)


def cost(flops, moved, transcendentals=0):
    return pl.CostEstimate(flops=flops, bytes_accessed=moved, transcendentals=transcendentals)


def run(kernel, name, grid, operands, in_specs, out_specs, out_shape, estimate, needs=(), through=(), scalars=(), fill=None):
    lead = len(scalars) + len(operands)
    extra = len(needs) + len(through)
    outs = len(out_shape)
    stay = pl.BlockSpec(memory_space=pltpu.HBM)
    aliases = {lead + len(needs) + place: outs + place for place in range(len(through))}
    for operand, out in (fill or {}).items():
        aliases[len(scalars) + operand] = out

    def body(*refs):
        kernel(*refs[:lead], *refs[lead + extra : lead + extra + outs])

    return pl.pallas_call(
        body,
        grid_spec=pltpu.PrefetchScalarGridSpec(
            num_scalar_prefetch=len(scalars),
            grid=grid,
            in_specs=list(in_specs) + [stay] * extra,
            out_specs=list(out_specs) + [stay] * len(through),
        ),
        out_shape=list(out_shape) + [jax.ShapeDtypeStruct(array.shape, array.dtype) for array in through],
        input_output_aliases=aliases,
        compiler_params=params(),
        cost_estimate=estimate,
        name=name,
    )(*scalars, *operands, *needs, *through)


def dot_nn(left, right):
    return lax.dot_general(left, right, (((1,), (0,)), ((), ())), preferred_element_type=jnp.float32)


def dot_nt(left, right):
    return lax.dot_general(left, right, (((1,), (1,)), ((), ())), preferred_element_type=jnp.float32)


def chunks(size, step):
    return [slice(start, start + step) for start in range(0, size, step)]


ROW_CHUNK = 256


def project_kernel(x_ref, first_ref, second_ref, bias_ref, out_ref):
    depth = first_ref.shape[0]
    for rows in chunks(x_ref.shape[0], ROW_CHUNK):
        total = dot_nn(x_ref[rows, :depth], first_ref[...]) + dot_nn(x_ref[rows, depth:], second_ref[...])
        out_ref[rows, :] = (total + bias_ref[...]).astype(out_ref.dtype)


def by_columns(array, tile):
    return pl.BlockSpec((array.shape[0], tile), lambda n, *_: (0, n))


def whole(array):
    return pl.BlockSpec(array.shape, lambda m, *_: (0,) * array.ndim)


def by_rows(array, tile):
    return pl.BlockSpec((tile, array.shape[1]), lambda m, *_: (m, 0))


def shaped(tokens, width, dtype):
    return jax.ShapeDtypeStruct((tokens, width), dtype)


def project(x, weight, bias, place):
    tokens, features = x.shape
    width = weight[0].shape[1] // 2
    tile = width // 2
    result = shaped(tokens, width, jnp.bfloat16)
    spec = pl.BlockSpec((weight[0].shape[0], tile), lambda n, *_: (0, 2 * n + place))
    return run(
        project_kernel,
        "project",
        (width // tile,),
        (x, *weight, bias),
        [whole(x), spec, spec, by_columns(bias, tile)],
        [by_columns(result, tile)],
        [result],
        cost(2 * tokens * features * width, 2 * (tokens * features + features * width + tokens * width)),
    )[0]


def gelu_parts(value):
    size = jnp.abs(value) * (0.5**0.5)
    near = 1.0 / (1.0 + 0.3275911 * size)
    bell = jnp.exp(-0.5 * value * value)
    series = near * (0.127414796 + near * (-0.142248368 + near * (0.7107068705 + near * (-0.7265760135 + near * 0.5307027145))))
    tail = series * bell
    below = jnp.where(value >= 0, 1.0 - tail, tail)
    return below, value * bell * 0.3989422804014327


def widen_kernel(x_ref, first_ref, second_ref, bias_ref, active_ref, slope_ref):
    depth = first_ref.shape[0]
    for rows in chunks(x_ref.shape[0], ROW_CHUNK):
        total = dot_nn(x_ref[rows, :depth], first_ref[...]) + dot_nn(x_ref[rows, depth:], second_ref[...])
        total = total + bias_ref[...]
        below, slope = gelu_parts(total)
        active_ref[rows, :] = (total * below).astype(jnp.bfloat16)
        slope_ref[rows, :] = (below + slope).astype(jnp.bfloat16)


def feed_in(x, weight, bias, tile, needs=(), through=()):
    tokens, features = x.shape
    width = weight[0].shape[1]
    result = shaped(tokens, width, jnp.bfloat16)
    return run(
        widen_kernel,
        "feed_in",
        (width // tile,),
        (x, *weight, bias),
        [whole(x), by_columns(weight[0], tile), by_columns(weight[1], tile), by_columns(bias, tile)],
        [by_columns(result, tile)] * 2,
        [result] * 2,
        cost(4 * tokens * features * width, 2 * (tokens * features + features * width + 2 * tokens * width)),
        needs,
        through,
    )


def unfeed_kernel(x_ref, first_ref, second_ref, slope_ref, out_ref, sum_ref):
    depth = first_ref.shape[0]
    column_sum = jnp.zeros(sum_ref.shape, jnp.float32)
    for rows in chunks(x_ref.shape[0], ROW_CHUNK):
        total = dot_nn(x_ref[rows, :depth], first_ref[...]) + dot_nn(x_ref[rows, depth:], second_ref[...])
        low = (total * slope_ref[rows, :].astype(jnp.float32)).astype(jnp.bfloat16)
        out_ref[rows, :] = low
        column_sum += jnp.sum(low.astype(jnp.float32), 0, keepdims=True)
    sum_ref[...] = column_sum


def feed_back(x, weight, slope, tile, needs=()):
    tokens, features = x.shape
    width = weight[0].shape[1]
    results = [shaped(tokens, width, jnp.bfloat16), shaped(1, width, jnp.float32)]
    return run(
        unfeed_kernel,
        "feed_back",
        (width // tile,),
        (x, *weight, slope),
        [whole(x), by_columns(weight[0], tile), by_columns(weight[1], tile), by_columns(slope, tile)],
        [by_columns(result, tile) for result in results],
        results,
        cost(2 * tokens * features * width, 2 * (tokens * features + features * width + 2 * tokens * width)),
        needs,
    )


def both_halves(x, first_ref, second_ref):
    return jnp.concatenate([dot_nt(x, first_ref[...]), dot_nt(x, second_ref[...])], 1)


def by_turns(x, first_ref, second_ref, place):
    half = x.shape[1] // 2
    parts = []
    for ref in (first_ref, second_ref):
        near = dot_nt(x[:, :half], ref[:, place * half : (place + 1) * half])
        parts.append(near + dot_nt(x[:, half:], ref[:, (2 + place) * half : (3 + place) * half]))
    return jnp.concatenate(parts, 1)


def layer_norm_rows(summed):
    center = jnp.mean(summed, 1, keepdims=True)
    shifted = summed - center
    inverse = lax.rsqrt(jnp.mean(shifted * shifted, 1, keepdims=True) + epsilon)
    return shifted * inverse, inverse


def layer_norm_back(gradient, normal, inverse, gain):
    scaled = gradient * gain
    first = jnp.mean(scaled, 1, keepdims=True)
    second = jnp.mean(scaled * normal, 1, keepdims=True)
    return inverse * (scaled - first - normal * second)


def attended_kernel(context_ref, first_ref, second_ref, x_ref, vector_ref, normal_ref, low_ref, inverse_ref):
    attended = by_turns(context_ref[...], first_ref, second_ref, 1) + vector_ref[0:1, :]
    normal, inverse = layer_norm_rows(x_ref[...].astype(jnp.float32) + attended)
    normal_ref[...] = normal
    low_ref[...] = (normal * vector_ref[1:2, :] + vector_ref[2:3, :]).astype(jnp.bfloat16)
    inverse_ref[...] = jnp.broadcast_to(inverse, inverse_ref.shape)


def attended_norm(context, weight, x, vectors, tile, needs=(), through=()):
    tokens, features = x.shape
    results = [
        shaped(tokens, features, jnp.float32),
        shaped(tokens, features, jnp.bfloat16),
        shaped(tokens, 128, jnp.float32),
    ]
    return run(
        attended_kernel,
        "attended_norm",
        (tokens // tile,),
        (context, *weight, x, vectors),
        [by_rows(context, tile), whole(weight[0]), whole(weight[1]), by_rows(x, tile), whole(vectors)],
        [by_rows(result, tile) for result in results],
        results,
        cost(2 * tokens * features * context.shape[1], 14 * tokens * features),
        needs,
        through,
    )


def fed_kernel(
    near_ref, far_ref, near0_ref, near1_ref, far0_ref, far1_ref, normal_ref, cotangent_ref, vector_ref, order_ref,
    out_ref, grad_ref, low_ref, sum_ref,
):
    fed = both_halves(near_ref[...], near0_ref, near1_ref) + both_halves(far_ref[...], far0_ref, far1_ref)
    fed = fed + vector_ref[3:4, :]
    hidden = normal_ref[...] * vector_ref[1:2, :] + vector_ref[2:3, :]
    normal, inverse = layer_norm_rows(hidden + fed)
    output = (normal * vector_ref[4:5, :] + vector_ref[5:6, :]).astype(jnp.bfloat16)
    out_ref[...] = dot_nt(output, order_ref[...]).astype(jnp.bfloat16)
    upstream = cotangent_ref[...].astype(jnp.float32)
    gradient = layer_norm_back(upstream, normal, inverse, vector_ref[4:5, :])
    grad_ref[...] = gradient
    low = gradient.astype(jnp.bfloat16)
    low_ref[...] = low

    @pl.when(pl.program_id(0) == 0)
    def clear():
        sum_ref[...] = jnp.zeros_like(sum_ref)

    sum_ref[0:1, :] += jnp.sum(upstream * normal, 0, keepdims=True)
    sum_ref[1:2, :] += jnp.sum(upstream, 0, keepdims=True)
    sum_ref[2:3, :] += jnp.sum(low.astype(jnp.float32), 0, keepdims=True)


def fed_norm(actives, weights, normal, cotangent, vectors, order, tile):
    tokens, features = normal.shape
    halves = [half for weight in weights for half in weight]
    results = [
        shaped(tokens, features, jnp.bfloat16),
        shaped(tokens, features, jnp.float32),
        shaped(tokens, features, jnp.bfloat16),
    ]
    sums = shaped(8, features, jnp.float32)
    units = 2 * actives[0].shape[1]
    return run(
        fed_kernel,
        "fed_norm",
        (tokens // tile,),
        (*actives, *halves, normal, cotangent, vectors, order),
        [by_rows(active, tile) for active in actives]
        + [whole(half) for half in halves]
        + [by_rows(normal, tile), by_rows(cotangent, tile), whole(vectors), whole(order)],
        [by_rows(result, tile) for result in results] + [whole(sums)],
        results + [sums],
        cost(2 * tokens * features * (units + features), 2 * units * (tokens + features) + 14 * tokens * features),
    )


def hidden_kernel(
    near_ref, far_ref, near0_ref, near1_ref, far0_ref, far1_ref, second_grad_ref, normal_ref, inverse_ref, vector_ref,
    grad_ref, low_ref, sum_ref,
):
    gradient = both_halves(near_ref[...], near0_ref, near1_ref) + both_halves(far_ref[...], far0_ref, far1_ref)
    gradient = gradient + second_grad_ref[...]
    normal = normal_ref[...]
    first = layer_norm_back(gradient, normal, inverse_ref[:, 0:1], vector_ref[1:2, :])
    grad_ref[...] = first
    low = first.astype(jnp.bfloat16)
    low_ref[...] = low

    @pl.when(pl.program_id(0) == 0)
    def clear():
        sum_ref[...] = jnp.zeros_like(sum_ref)

    sum_ref[0:1, :] += jnp.sum(gradient * normal, 0, keepdims=True)
    sum_ref[1:2, :] += jnp.sum(gradient, 0, keepdims=True)
    sum_ref[2:3, :] += jnp.sum(low.astype(jnp.float32), 0, keepdims=True)


def hidden_back(pre_grads, weights, second_grad, normal, inverse, vectors, tile, needs=()):
    tokens, features = normal.shape
    halves = [half for weight in weights for half in weight]
    results = [shaped(tokens, features, jnp.float32), shaped(tokens, features, jnp.bfloat16)]
    sums = shaped(8, features, jnp.float32)
    units = 2 * pre_grads[0].shape[1]
    return run(
        hidden_kernel,
        "hidden_back",
        (tokens // tile,),
        (*pre_grads, *halves, second_grad, normal, inverse, vectors),
        [by_rows(pre_grad, tile) for pre_grad in pre_grads]
        + [whole(half) for half in halves]
        + [by_rows(second_grad, tile), by_rows(normal, tile), by_rows(inverse, tile), whole(vectors)],
        [by_rows(result, tile) for result in results] + [whole(sums)],
        results + [sums],
        cost(2 * tokens * features * units, 2 * units * (tokens + features) + 14 * tokens * features),
        needs,
    )


def tokens_kernel(dq_ref, dk_ref, dv_ref, qk0_ref, qk1_ref, vo0_ref, vo1_ref, first_ref, order_ref, out_ref):
    total = (
        by_turns(dq_ref[...], qk0_ref, qk1_ref, 0)
        + by_turns(dk_ref[...], qk0_ref, qk1_ref, 1)
        + by_turns(dv_ref[...], vo0_ref, vo1_ref, 0)
        + first_ref[...]
    )
    out_ref[...] = dot_nt(total.astype(jnp.bfloat16), order_ref[...]).astype(jnp.bfloat16)


def tokens_back(grads, weights, first_grad, order, tile, needs=()):
    tokens, features = first_grad.shape
    halves = [half for weight in weights for half in weight]
    result = shaped(tokens, features, jnp.bfloat16)
    return run(
        tokens_kernel,
        "tokens_back",
        (tokens // tile,),
        (*grads, *halves, first_grad, order),
        [by_rows(grad, tile) for grad in grads]
        + [whole(half) for half in halves]
        + [by_rows(first_grad, tile), whole(order)],
        [by_rows(result, tile)],
        [result],
        cost(8 * tokens * features * features, 20 * tokens * features),
        needs,
    )


def key_bias(length, keys):
    place = lax.broadcasted_iota(jnp.int32, (keys, 1), 0)
    return jnp.where(place < length, 0.0, masked_score)


def attend_kernel(length_ref, q_ref, k_ref, v_ref, context_ref, logsum_ref):
    bias = key_bias(length_ref[pl.program_id(0)], k_ref.shape[0])
    queries = q_ref[...] * (HEAD_DIM**-0.5)
    key_rows = k_ref[...]
    values = v_ref[...].T
    lane = lax.broadcasted_iota(jnp.int32, queries.shape, 1) // HEAD_DIM
    parts = []
    for head in range(queries.shape[1] // HEAD_DIM):
        one = jnp.where(lane == head, queries, jnp.zeros_like(queries))
        scores = dot_nt(key_rows, one) + bias
        top = jnp.max(scores, 0, keepdims=True)
        raised = jnp.exp(scores - top)
        total = jnp.sum(raised, 0, keepdims=True)
        logsum_ref[0, head : head + 1, :] = top + jnp.log(total)
        mixed = dot_nn(values[head * HEAD_DIM : (head + 1) * HEAD_DIM, :], raised.astype(jnp.bfloat16))
        parts.append(mixed / total)
    context_ref[...] = jnp.concatenate(parts, 0).T.astype(jnp.bfloat16)


def attend(queries, key_rows, values, lengths, needs=(), through=()):
    tokens, features = queries.shape
    sequences = lengths.shape[0]
    wide = 2 * HEAD_DIM
    spec = pl.BlockSpec((SEQ_LEN, wide), lambda s, h, _: (s, h))
    steps = features // wide
    return run(
        attend_kernel,
        "attend",
        (sequences, steps),
        (queries, key_rows, values),
        [spec] * 3,
        [spec, pl.BlockSpec((1, 8, SEQ_LEN), lambda s, h, _: (s * steps + h, 0, 0))],
        [shaped(tokens, features, jnp.bfloat16), jax.ShapeDtypeStruct((sequences * steps, 8, SEQ_LEN), jnp.float32)],
        cost(16 * tokens * features * SEQ_LEN, 8 * tokens * features),
        needs,
        through,
        (lengths,),
    )


def attend_back_kernel(length_ref, q_ref, k_ref, v_ref, grad_ref, logsum_ref, dq_ref, dk_ref, dv_ref, sum_ref):
    bias = key_bias(length_ref[pl.program_id(0)], k_ref.shape[0])
    queries = q_ref[...] * (HEAD_DIM**-0.5)
    key_rows = k_ref[...]
    key_columns = key_rows.T
    values = v_ref[...]
    grads = grad_ref[...]
    lane = lax.broadcasted_iota(jnp.int32, queries.shape, 1) // HEAD_DIM
    query_parts = []
    key_grad = jnp.zeros(queries.shape, jnp.float32)
    value_grad = jnp.zeros(queries.shape, jnp.float32)
    for head in range(queries.shape[1] // HEAD_DIM):
        one = jnp.where(lane == head, queries, jnp.zeros_like(queries))
        one_grad = jnp.where(lane == head, grads, jnp.zeros_like(grads))
        chances = jnp.exp(dot_nt(key_rows, one) + bias - logsum_ref[0, head : head + 1, :])
        chance_grad = dot_nt(values, one_grad)
        value_grad += dot_nn(chances.astype(jnp.bfloat16), one_grad)
        inner = jnp.sum(chances * chance_grad, 0, keepdims=True)
        score_grad = (chances * (chance_grad - inner)).astype(jnp.bfloat16)
        key_grad += dot_nn(score_grad, one)
        query_parts.append(dot_nn(key_columns[head * HEAD_DIM : (head + 1) * HEAD_DIM, :], score_grad))
    query_grad = jnp.concatenate(query_parts, 0) * (HEAD_DIM**-0.5)
    query_grad = query_grad.T.astype(jnp.bfloat16)
    value_grad = value_grad.astype(jnp.bfloat16)
    dq_ref[...] = query_grad
    dk_ref[...] = key_grad.astype(jnp.bfloat16)
    dv_ref[...] = value_grad
    sum_ref[...] = jnp.zeros_like(sum_ref)
    sum_ref[0, 0:1, :] = jnp.sum(query_grad.astype(jnp.float32), 0, keepdims=True)
    sum_ref[0, 1:2, :] = jnp.sum(value_grad.astype(jnp.float32), 0, keepdims=True)


def attend_grads(queries, key_rows, values, context_grad, logsums, lengths, part, filled=(), needs=()):
    tokens, features = queries.shape
    sequences = lengths.shape[0]
    wide = 2 * HEAD_DIM
    steps = features // wide
    count = steps // 2
    first = part * count
    spec = pl.BlockSpec((SEQ_LEN, wide), lambda s, h, _: (s, first + h))
    sums_spec = pl.BlockSpec((1, 8, wide), lambda s, h, _: (s, 0, first + h))
    results = [shaped(tokens, features, jnp.bfloat16)] * 3
    results = results + [jax.ShapeDtypeStruct((sequences, 8, features), jnp.float32)]

    def kernel(*refs):
        attend_back_kernel(*refs[:6], *refs[6 + len(filled) :])

    return run(
        kernel,
        "attend_grads",
        (sequences, count),
        (queries, key_rows, values, context_grad, logsums, *filled),
        [spec] * 4
        + [pl.BlockSpec((1, 8, SEQ_LEN), lambda s, h, _: (s * steps + first + h, 0, 0))]
        + [pl.BlockSpec(memory_space=pltpu.HBM)] * len(filled),
        [spec] * 3 + [sums_spec],
        results,
        cost(20 * tokens * features * SEQ_LEN, 7 * tokens * features),
        needs,
        (),
        (lengths,),
        {5 + place: place for place in range(len(filled))},
    )


def weight_grad(left, right):
    half = left.shape[1] // 2

    def part(columns):
        return lax.dot_general(left[:, columns], right, (((0,), (0,)), ((), ())), preferred_element_type=jnp.float32)

    return part(slice(0, half)), part(slice(half, 2 * half)).astype(jnp.bfloat16)


def by_tokens(
    tokens,
    qkv_weight,
    qv_bias,
    out_weight,
    out_bias,
    norm1_gain,
    norm1_shift,
    in_weight,
    in_bias,
    down_weight,
    down_bias,
    norm2_gain,
    norm2_shift,
    lengths,
    cotangent,
):
    rows = lax.axis_size("row")
    row, col = lax.axis_index("row"), lax.axis_index("col")
    local_width = tokens.shape[1]
    features = 2 * local_width
    share = tokens.shape[0] // 2
    bits = [1 << level for level in range(1, rows.bit_length() - 1)]
    cross, line = bits[0], bits[:0:-1]
    via_col = line + [cross, 0]
    via_row = line + [0, cross]

    levels = len(line)
    units = in_weight.shape[1] // 2
    tokens_far = hop(lax.dynamic_slice_in_dim(tokens, (1 - col) * share, share, 0), "col", 1, 2)
    small = jnp.stack([out_bias, norm1_gain, norm1_shift, down_bias, norm2_gain, norm2_shift, qv_bias[0], qv_bias[1]])
    small = jnp.concatenate([small, in_bias.reshape(-1, local_width)], 0)
    qk = Gather(jnp.concatenate([qkv_weight[:, 0], qkv_weight[:, 1]], 1), via_col, rows)
    vo = Gather(jnp.concatenate([qkv_weight[:, 2], out_weight], 1), via_row, rows)
    in_near, in_far = (
        Gather(in_weight[:, :units], via_col, rows),
        Gather(in_weight[:, units:], via_row, rows),
    )
    down_near, down_far = (
        Gather(down_weight[:, :units], via_col, rows),
        Gather(down_weight[:, units:], via_row, rows),
    )
    qk.start()
    vo.start()
    far = hop(small, "col", 1, 2)
    order = order_matrix(row, col, rows, features)
    for step in range(levels - 1):
        order = point(order, [qk, vo], [qk, vo])
    order = point(order, [qk, vo], [qk, vo, in_near, in_far])
    tokens_near = lax.dynamic_slice_in_dim(tokens, col * share, share, 0)
    x = dot_nn(jnp.concatenate([tokens_near, tokens_far], 1), order).astype(jnp.bfloat16)
    for step in range(levels - 1):
        x = point(x, [in_near, in_far], [in_near, in_far])
    x = point(x, [qk, vo], [qk, vo])
    x = point(x, [in_near, in_far], [down_near, down_far])
    for step in range(levels - 1):
        x = point(x, [down_near, down_far], [down_near, down_far])
    x = point(x, [qk, vo], [qk, vo, in_near, in_far])
    qk_full, vo_full = qk.both(), vo.both()

    pair = jnp.concatenate([small, far], 1)
    straight = jnp.where(col == 0, pair[:6], jnp.concatenate([far[:6], small[:6]], 1))
    vectors = jnp.pad(to_relative(straight, row, rows), ((0, 2), (0, 0)))
    in_biases = [
        jnp.concatenate([one.reshape(2, 1, -1)[half] for one in (small[8:], far[8:])], 1) for half in range(2)
    ]
    own_lengths = lax.dynamic_slice_in_dim(lengths, col * (lengths.shape[0] // 2), lengths.shape[0] // 2)
    no_bias = jnp.zeros((1, features), jnp.float32)

    queries = project(x, qk_full, pair[6:7], 0)
    key_rows = project(x, qk_full, no_bias, 1)
    values = project(x, vo_full, pair[7:8], 0)
    values = point(values, [in_near, in_far, down_near, down_far], [in_near, in_far])
    context, logsums = attend(queries, key_rows, values, own_lengths)
    context = point(context, [in_near, in_far], [in_near, in_far, down_near, down_far])
    cotangent_far = lax.dynamic_slice_in_dim(cotangent, (1 - col) * share, share, 0)
    context, cotangent_far = lax.optimization_barrier((context, cotangent_far))
    cotangent_far = hop(cotangent_far, "col", 1, 2)
    normal_one, hidden_low, inverse_one = attended_norm(context, vo_full, x, vectors, 256)
    in_full = [in_near.both(), in_far.both()]
    active_near, slope_near = feed_in(hidden_low, in_full[0], in_biases[0], 512)
    hidden_low, active_near, cotangent_far = lax.optimization_barrier((hidden_low, active_near, cotangent_far))
    cotangent_near = lax.dynamic_slice_in_dim(cotangent, col * share, share, 0)
    hidden_low = point(hidden_low, [down_near, down_far], [down_near, down_far])
    active_far, slope_far = feed_in(hidden_low, in_full[1], in_biases[1], 512)
    active_far = point(active_far, [down_near, down_far], [down_near, down_far])
    down_full = [down_near.both(), down_far.both()]
    upstream = dot_nn(jnp.concatenate([cotangent_near, cotangent_far], 1), order).astype(jnp.bfloat16)
    output, grad_second, grad_fed, sums_two = fed_norm(
        (active_near, active_far), down_full, normal_one, upstream, vectors, order, 256
    )

    half = local_width
    output_far = hop(output[:, half:], "col", 1, 2)
    back = line[::-1]
    by_cross, by_col = [cross, 0] + back, [0, cross] + back
    down_parts = [weight_grad(grad_fed, active) for active in (active_near, active_far)]
    downs = [Scatter(parts, path, rows) for parts, path in zip(down_parts, (by_cross, by_col))]
    pre_near, sum_near = feed_back(grad_fed, down_full[0], slope_near, 512, [sent for _, sent in down_parts])
    pre_far, sum_far = feed_back(grad_fed, down_full[1], slope_far, 512)
    pre_far = point(pre_far, downs, downs)
    in_parts = [weight_grad(hidden_low, pre_grad) for pre_grad in (pre_near, pre_far)]
    ins = [Scatter(parts, path, rows) for parts, path in zip(in_parts, (by_cross, by_col))]
    grad_first, grad_attended, sums_one = hidden_back(
        (pre_near, pre_far), in_full, grad_second, normal_one, inverse_one, vectors, 256,
        [down.held for down in downs] + [sent for _, sent in in_parts],
    )
    grad_attended = point(grad_attended, ins + downs, ins + downs)
    out_parts = weight_grad(grad_attended, context)
    outs = [Scatter(out_parts, back + [cross, 0], rows)]
    grad_attended, _ = lax.optimization_barrier((grad_attended, out_parts[1]))
    context_grad = project(grad_attended, vo_full, no_bias, 1)
    context_grad = point(context_grad, outs, outs)
    attention = (queries, key_rows, values)
    near_grads = list(attend_grads(*attention, context_grad, logsums, own_lengths, 1))
    near_grads[0] = point(near_grads[0], outs, outs)
    dq, dk, dv, qv_sums = attend_grads(*attention, context_grad, logsums, own_lengths, 0, near_grads)
    def straighten(array):
        split = array.reshape(array.shape[0], 2, -1)
        return jnp.where(col == 0, split, jnp.flip(split, 1)).reshape(array.shape[0], -1)

    def own(array):
        return lax.dynamic_slice_in_dim(array, col * (array.shape[1] // 2), array.shape[1] // 2, 1)

    feature_sums = from_relative(jnp.concatenate([sums_two[:3], sums_one[:3]], 0), row, rows)
    unit_sums = straighten(jnp.concatenate([sum_near, sum_far], 0))
    qv_sums = straighten(jnp.sum(qv_sums, 0)[:2])
    sums = jnp.concatenate([feature_sums, unit_sums.reshape(-1, features), qv_sums], 0)
    sums = lax.all_gather(sums, ("row", "col"))
    output_far, dv = lax.optimization_barrier((output_far, dv))
    dv = point(dv, ins + downs + outs, ins + downs + outs)
    value_parts = weight_grad(x, dv)
    turns = jnp.concatenate([dq[:, :half], dk[:, :half], dq[:, half:], dk[:, half:]], 1)
    pair_parts = weight_grad(x, turns)
    pairs, lone = [Scatter(pair_parts, by_cross, rows)], [Scatter(value_parts, back + [0, cross], rows)]
    dv = point(dv, pairs + lone, pairs + lone)
    (tokens_grad,) = tokens_back((dq, dk, dv), (qk_full, vo_full), grad_first, order, 256)
    tokens_grad = point(tokens_grad, downs + outs, downs + outs)
    tokens_mine = tokens_grad[:, :half]
    tokens_far = hop(tokens_grad[:, half:], "col", 1, 2)
    later = ins + downs + outs + lone + pairs
    tokens_mine = point(tokens_mine, lone, lone)
    tokens_mine = point(tokens_mine, ins + outs, ins + outs)
    tokens_mine = point(tokens_mine, pairs, pairs)
    tokens_mine = point(tokens_mine, downs + lone, downs + lone)
    while any(chain.order for chain in later):
        moving = [chain for chain in later if chain.order]
        tokens_mine = point(tokens_mine, moving, [chain for chain in moving if len(chain.order) > 1])
    turned = pairs[0].result()

    def give(mine, arrived):
        return jnp.where(col == 0, jnp.concatenate([mine, arrived], 0), jnp.concatenate([arrived, mine], 0))

    sums, tokens_mine = lax.optimization_barrier((sums, tokens_mine))
    sums = jnp.sum(sums, 0)
    feature_sums = own(sums[:6])
    in_bias_grad = own(sums[6:-2].reshape(2, -1)).reshape(-1)
    return (
        give(output[:, :half], output_far),
        give(tokens_mine, tokens_far).astype(jnp.float32),
        jnp.stack([turned[:, :half], turned[:, half:], lone[0].result()], 1),
        own(sums[-2:]),
        outs[0].result(),
        feature_sums[5],
        feature_sums[3],
        feature_sums[4],
        jnp.concatenate([chain.result() for chain in ins], 1),
        in_bias_grad,
        jnp.concatenate([chain.result() for chain in downs], 1),
        feature_sums[2],
        feature_sums[0],
        feature_sums[1],
    )


def device_program(*arrays):
    rows, cols = lax.axis_size("row"), lax.axis_size("col")
    sequences = arrays[13].shape[0]
    if cols == 2 and rows >= 8 and rows & (rows - 1) == 0 and sequences % 2 == 0:
        return by_tokens(*arrays)
    return on_device(*arrays)


def solution(mesh):
    placed = (
        P("row", "col"),
        P("row", None, "col"),
        P(None, "col"),
        P("row", "col"),
        P("col"),
        P("col"),
        P("col"),
        P("row", "col"),
        P("col"),
        P("row", "col"),
        P("col"),
        P("col"),
        P("col"),
        P("row"),
        P("row", "col"),
    )
    return jax.shard_map(
        device_program,
        mesh=mesh,
        in_specs=placed,
        out_specs=(
            P("row", "col"),
            P("row", "col"),
            P("row", None, "col"),
            P(None, "col"),
            P("row", "col"),
            P("col"),
            P("col"),
            P("col"),
            P("row", "col"),
            P("col"),
            P("row", "col"),
            P("col"),
            P("col"),
            P("col"),
        ),
        check_vma=False,
    )
```

```python
import jax
import jax.numpy as jnp
from jax import lax
from jax.experimental import pallas as pl
from jax.experimental.pallas import tpu as pltpu
from jax.sharding import PartitionSpec as P

HEAD_DIM = 64
SEQ_LEN = 512


epsilon = 1e-05
masked_score = -1000000000.0


def widen(portion):
    return lax.all_gather(portion, "col", axis=1, tiled=True)


def widen_grad(portion):
    return lax.all_gather(portion, "col", axis=1, tiled=True)


def reduce_out(partial_rows):
    return lax.psum_scatter(partial_rows, "col", scatter_dimension=1, tiled=True)


def reduce_grad(partial_rows):
    return lax.psum_scatter(partial_rows, "col", scatter_dimension=1, tiled=True)


def exact_gelu(values):
    return jax.nn.gelu(values, approximate=False)


def normalize(summed, norm_gain, norm_shift, features):
    moments = lax.psum((jnp.sum(summed, 1), jnp.sum(summed * summed, 1)), "col")
    center = moments[0] / features
    inverse = lax.rsqrt(moments[1] / features - center * center + epsilon)
    normal = (summed - center[:, None]) * inverse[:, None]
    return (normal * norm_gain + norm_shift, normal, inverse)


def normalize_back(gradient, normal, inverse, norm_gain, features):
    scaled = gradient * norm_gain
    moments = lax.psum((jnp.sum(scaled, 1), jnp.sum(scaled * normal, 1)), "col")
    return inverse[:, None] * (
        scaled - moments[0][:, None] / features - normal * moments[1][:, None] / features
    )


def masked_scores(queries, key_rows, length):
    factor = HEAD_DIM ** (-0.5)
    scores = (
        jnp.einsum("qhd,khd->hqk", queries, key_rows, preferred_element_type=jnp.float32) * factor
    )
    usable = jnp.arange(scores.shape[2]) < length
    return jnp.where(usable[None, None, :], scores, masked_score)


def attend_forward(element):
    queries, key_rows, values, length = element
    scores = masked_scores(queries, key_rows, length)
    highest = jnp.max(scores, 2, keepdims=True)
    raised = jnp.exp(scores - highest)
    row_total = jnp.sum(raised, 2, keepdims=True)
    chances = (raised / row_total).astype(jnp.bfloat16)
    context = jnp.einsum("hqk,khd->qhd", chances, values, preferred_element_type=jnp.float32)
    return (context.astype(jnp.bfloat16), (highest + jnp.log(row_total))[:, :, 0])


def attend_back(element):
    queries, key_rows, values, context_grad, logsum, length = element
    factor = HEAD_DIM ** (-0.5)
    scores = masked_scores(queries, key_rows, length)
    chances = jnp.exp(scores - logsum[:, :, None])
    chance_grad = jnp.einsum(
        "qhd,khd->hqk", context_grad, values, preferred_element_type=jnp.float32
    )
    value_grad = jnp.einsum(
        "hqk,qhd->khd",
        chances.astype(jnp.bfloat16),
        context_grad,
        preferred_element_type=jnp.float32,
    )
    inner = jnp.sum(chances * chance_grad, 2, keepdims=True)
    score_grad = (chances * (chance_grad - inner)).astype(jnp.bfloat16)
    query_grad = (
        jnp.einsum("hqk,khd->qhd", score_grad, key_rows, preferred_element_type=jnp.float32)
        * factor
    )
    key_grad = (
        jnp.einsum("hqk,qhd->khd", score_grad, queries, preferred_element_type=jnp.float32) * factor
    )
    return jnp.stack([query_grad, key_grad, value_grad], 1).astype(jnp.bfloat16)


def on_device(
    tokens,
    qkv_weight,
    qv_bias,
    out_weight,
    out_bias,
    norm1_gain,
    norm1_shift,
    in_weight,
    in_bias,
    down_weight,
    down_bias,
    norm2_gain,
    norm2_shift,
    lengths,
    cotangent,
):
    local_width = tokens.shape[1]
    features = local_width * lax.axis_size("col")
    token_count = tokens.shape[0]
    sequences = lengths.shape[0]
    heads_here = local_width // HEAD_DIM
    qkv_full, out_full, in_full, down_full = (
        lax.all_gather(qkv_weight, "row", axis=0, tiled=True),
        lax.all_gather(out_weight, "row", axis=0, tiled=True),
        lax.all_gather(in_weight, "row", axis=0, tiled=True),
        lax.all_gather(down_weight, "row", axis=0, tiled=True),
    )
    tokens_full = widen(tokens)
    projected = jnp.einsum("td,dsf->tsf", tokens_full, qkv_full, preferred_element_type=jnp.float32)
    qkv_bias = jnp.stack([qv_bias[0], jnp.zeros_like(qv_bias[0]), qv_bias[1]])
    qkv_rows = (projected + qkv_bias).astype(jnp.bfloat16)
    split_rows = qkv_rows.reshape(sequences, SEQ_LEN, 3, heads_here, HEAD_DIM)
    queries = split_rows[:, :, 0]
    key_rows = split_rows[:, :, 1]
    values = split_rows[:, :, 2]
    context, logsums = lax.map(attend_forward, (queries, key_rows, values, lengths))
    context = context.reshape(token_count, local_width)
    attended = (
        reduce_out(jnp.einsum("tf,of->to", context, out_full, preferred_element_type=jnp.float32))
        + out_bias
    )
    first_sum = tokens.astype(jnp.float32) + attended
    hidden_one, normal_one, inverse_one = normalize(first_sum, norm1_gain, norm1_shift, features)
    hidden_low = hidden_one.astype(jnp.bfloat16)
    hidden_full = widen(hidden_low)
    pre_act = jnp.dot(hidden_full, in_full, preferred_element_type=jnp.float32) + in_bias
    activated = exact_gelu(pre_act).astype(jnp.bfloat16)
    fed = (
        reduce_out(
            jnp.einsum("tf,of->to", activated, down_full, preferred_element_type=jnp.float32)
        )
        + down_bias
    )
    second_sum = hidden_one + fed
    output, normal_two, inverse_two = normalize(second_sum, norm2_gain, norm2_shift, features)
    qkv_full, out_full, in_full, down_full = (
        lax.all_gather(qkv_weight, "row", axis=0, tiled=True),
        lax.all_gather(out_weight, "row", axis=0, tiled=True),
        lax.all_gather(in_weight, "row", axis=0, tiled=True),
        lax.all_gather(down_weight, "row", axis=0, tiled=True),
    )
    tokens_full, hidden_full = (
        lax.all_gather(tokens, "col", axis=1, tiled=True),
        lax.all_gather(hidden_low, "col", axis=1, tiled=True),
    )
    upstream = cotangent.astype(jnp.float32)
    gain_two_grad = jnp.sum(upstream * normal_two, 0)
    shift_two_grad = jnp.sum(upstream, 0)
    grad_second = normalize_back(upstream, normal_two, inverse_two, norm2_gain, features)
    grad_fed = grad_second.astype(jnp.bfloat16)
    down_bias_grad = jnp.sum(grad_fed.astype(jnp.float32), 0)
    fed_full = widen_grad(grad_fed)
    down_grad = jnp.einsum("to,tf->of", fed_full, activated, preferred_element_type=jnp.float32)
    act_grad = jnp.dot(fed_full, down_full, preferred_element_type=jnp.float32)
    unused_value, gelu_pull = jax.vjp(exact_gelu, pre_act)
    pre_grad = gelu_pull(act_grad)[0].astype(jnp.bfloat16)
    in_bias_grad = jnp.sum(pre_grad.astype(jnp.float32), 0)
    in_grad = jnp.einsum("td,tf->df", hidden_full, pre_grad, preferred_element_type=jnp.float32)
    hidden_grad = (
        reduce_grad(jnp.einsum("tf,df->td", pre_grad, in_full, preferred_element_type=jnp.float32))
        + grad_second
    )
    gain_one_grad = jnp.sum(hidden_grad * normal_one, 0)
    shift_one_grad = jnp.sum(hidden_grad, 0)
    grad_first = normalize_back(hidden_grad, normal_one, inverse_one, norm1_gain, features)
    grad_attended = grad_first.astype(jnp.bfloat16)
    out_bias_grad = jnp.sum(grad_attended.astype(jnp.float32), 0)
    attended_full = widen_grad(grad_attended)
    out_grad = jnp.einsum("to,tf->of", attended_full, context, preferred_element_type=jnp.float32)
    context_grad = jnp.dot(attended_full, out_full, preferred_element_type=jnp.float32).astype(
        jnp.bfloat16
    )
    context_split = context_grad.reshape(sequences, SEQ_LEN, heads_here, HEAD_DIM)
    qkv_grads = lax.map(attend_back, (queries, key_rows, values, context_split, logsums, lengths))
    qkv_grads = qkv_grads.reshape(token_count, 3, local_width)
    grad_float = qkv_grads.astype(jnp.float32)
    qv_bias_grad = jnp.stack([jnp.sum(grad_float[:, 0], 0), jnp.sum(grad_float[:, 2], 0)])
    qkv_grad = jnp.einsum("td,tsf->dsf", tokens_full, qkv_grads, preferred_element_type=jnp.float32)
    tokens_grad = (
        reduce_grad(
            jnp.einsum("tsf,dsf->td", qkv_grads, qkv_full, preferred_element_type=jnp.float32)
        )
        + grad_first
    )
    weight_grads = (
        lax.psum_scatter(
            qkv_grad.astype(jnp.bfloat16), "row", scatter_dimension=0, tiled=True
        ).astype(jnp.float32),
        lax.psum_scatter(
            out_grad.astype(jnp.bfloat16), "row", scatter_dimension=0, tiled=True
        ).astype(jnp.float32),
        lax.psum_scatter(
            in_grad.astype(jnp.bfloat16), "row", scatter_dimension=0, tiled=True
        ).astype(jnp.float32),
        lax.psum_scatter(
            down_grad.astype(jnp.bfloat16), "row", scatter_dimension=0, tiled=True
        ).astype(jnp.float32),
    )
    small_grads = lax.psum(
        (
            qv_bias_grad,
            out_bias_grad,
            gain_one_grad,
            shift_one_grad,
            in_bias_grad,
            down_bias_grad,
            gain_two_grad,
            shift_two_grad,
        ),
        "row",
    )
    return (
        output.astype(jnp.bfloat16),
        tokens_grad,
        weight_grads[0],
        small_grads[0],
        weight_grads[1],
        small_grads[1],
        small_grads[2],
        small_grads[3],
        weight_grads[2],
        small_grads[4],
        weight_grads[3],
        small_grads[5],
        small_grads[6],
        small_grads[7],
    )


def hop(array, axis, bit, size):
    return lax.ppermute(array, axis, [(place, place ^ bit) for place in range(size)])


def block_axis(bit, rows):
    return (rows // bit).bit_length() - 2


class Gather:
    def __init__(self, shard, order, rows):
        self.order, self.rows = list(order), rows
        self.held = shard.reshape((1,) * (rows.bit_length() - 2) + shard.shape)
        self.flight = None

    def start(self):
        if not self.order:
            self.held = self.held.reshape(-1, self.held.shape[-1])
            self.flight = hop(self.held, "row", 1, self.rows)
        elif self.order[0] == 0:
            self.flight = hop(self.held, "col", 1, 2)
        else:
            self.flight = hop(self.held, "row", self.order[0], self.rows)

    def land(self):
        bit = self.order.pop(0)
        axis = -1 if bit == 0 else block_axis(bit, self.rows)
        self.held = jnp.concatenate([self.held, self.flight], axis=axis)

    def both(self):
        return self.held, self.flight


class Scatter:
    def __init__(self, parts, order, rows):
        self.order, self.rows = [1, *order], rows
        self.mine, other = parts
        self.flight = hop(other, "row", 1, rows)

    def land(self):
        levels = self.rows.bit_length() - 2
        self.order.pop(0)
        self.total = self.mine + self.flight.astype(jnp.float32)
        self.held = self.total.astype(jnp.bfloat16)
        if self.held.ndim == 2:
            self.held = self.held.reshape((2,) * levels + (-1, self.held.shape[-1]))

    def start(self):
        if not self.order:
            return
        bit = self.order[0]
        axis = self.held.ndim - 1 if bit == 0 else block_axis(bit, self.rows)
        half = self.held.shape[axis] // 2
        self.mine = lax.slice_in_dim(self.held, 0, half, axis=axis).astype(jnp.float32)
        other = lax.slice_in_dim(self.held, half, 2 * half, axis=axis)
        self.flight = hop(other, "col", 1, 2) if bit == 0 else hop(other, "row", bit, self.rows)

    def result(self):
        return self.total.reshape(-1, self.total.shape[-1])


def tie(value, chains, name):
    tied = lax.optimization_barrier((value, *[getattr(chain, name) for chain in chains]))
    for chain, array in zip(chains, tied[1:]):
        setattr(chain, name, array)
    return tied[0]


def point(value, land=(), start=()):
    land = [chain for chain in land if chain.order]
    if land:
        value = tie(value, land, "flight")
        for chain in land:
            chain.land()
    if start:
        value = tie(value, start, "held")
        for chain in start:
            chain.start()
    return value


def relative_blocks(vectors, row, rows):
    levels = rows.bit_length() - 1
    count = vectors.shape[0]
    split = vectors.reshape((count,) + (2,) * levels + (-1,))
    for level in range(levels):
        flag = (row >> (levels - 1 - level)) & 1
        split = jnp.where(flag == 1, jnp.flip(split, 1 + level), split)
    return split


def to_relative(vectors, row, rows):
    split = relative_blocks(vectors, row, rows)
    levels = rows.bit_length() - 1
    return jnp.moveaxis(split, levels, 1).reshape(vectors.shape)


def from_relative(vectors, row, rows):
    levels = rows.bit_length() - 1
    count = vectors.shape[0]
    split = vectors.reshape((count,) + (2,) * levels + (-1,))
    split = jnp.moveaxis(split, 1, levels).reshape(vectors.shape)
    return relative_blocks(split, row, rows).reshape(vectors.shape)


def order_matrix(row, col, rows, features):
    block = features // rows
    half = features // 2
    came = lax.broadcasted_iota(jnp.int32, (features, features), 0)
    came = jnp.where(came < half, came + col * half, came - half + (1 - col) * half)
    goes = lax.broadcasted_iota(jnp.int32, (features, features), 1)
    place = goes // block
    low = place // (rows // 2)
    natural = (place % (rows // 2)) * 2 + low
    goes = (natural ^ row) * block + goes % block
    return (came == goes).astype(jnp.bfloat16)


def params(limit_mib=48):
    return pltpu.CompilerParams(vmem_limit_bytes=limit_mib * 2**20)


def cost(flops, moved, transcendentals=0):
    return pl.CostEstimate(flops=flops, bytes_accessed=moved, transcendentals=transcendentals)


def run(kernel, name, grid, operands, in_specs, out_specs, out_shape, estimate, needs=(), through=(), scalars=(), fill=None):
    lead = len(scalars) + len(operands)
    extra = len(needs) + len(through)
    outs = len(out_shape)
    stay = pl.BlockSpec(memory_space=pltpu.HBM)
    aliases = {lead + len(needs) + place: outs + place for place in range(len(through))}
    for operand, out in (fill or {}).items():
        aliases[len(scalars) + operand] = out

    def body(*refs):
        kernel(*refs[:lead], *refs[lead + extra : lead + extra + outs])

    return pl.pallas_call(
        body,
        grid_spec=pltpu.PrefetchScalarGridSpec(
            num_scalar_prefetch=len(scalars),
            grid=grid,
            in_specs=list(in_specs) + [stay] * extra,
            out_specs=list(out_specs) + [stay] * len(through),
        ),
        out_shape=list(out_shape) + [jax.ShapeDtypeStruct(array.shape, array.dtype) for array in through],
        input_output_aliases=aliases,
        compiler_params=params(),
        cost_estimate=estimate,
        name=name,
    )(*scalars, *operands, *needs, *through)


def dot_nn(left, right):
    return lax.dot_general(left, right, (((1,), (0,)), ((), ())), preferred_element_type=jnp.float32)


def dot_nt(left, right):
    return lax.dot_general(left, right, (((1,), (1,)), ((), ())), preferred_element_type=jnp.float32)


def chunks(size, step):
    return [slice(start, start + step) for start in range(0, size, step)]


ROW_CHUNK = 256


def project_kernel(x_ref, first_ref, second_ref, bias_ref, out_ref):
    depth = first_ref.shape[0]
    for rows in chunks(x_ref.shape[0], ROW_CHUNK):
        total = dot_nn(x_ref[rows, :depth], first_ref[...]) + dot_nn(x_ref[rows, depth:], second_ref[...])
        out_ref[rows, :] = (total + bias_ref[...]).astype(out_ref.dtype)


def by_columns(array, tile):
    return pl.BlockSpec((array.shape[0], tile), lambda n, *_: (0, n))


def whole(array):
    return pl.BlockSpec(array.shape, lambda m, *_: (0,) * array.ndim)


def by_rows(array, tile):
    return pl.BlockSpec((tile, array.shape[1]), lambda m, *_: (m, 0))


def shaped(tokens, width, dtype):
    return jax.ShapeDtypeStruct((tokens, width), dtype)


def project(x, weight, bias, place):
    tokens, features = x.shape
    width = weight[0].shape[1] // 2
    tile = width // 2
    result = shaped(tokens, width, jnp.bfloat16)
    spec = pl.BlockSpec((weight[0].shape[0], tile), lambda n, *_: (0, 2 * n + place))
    return run(
        project_kernel,
        "project",
        (width // tile,),
        (x, *weight, bias),
        [whole(x), spec, spec, by_columns(bias, tile)],
        [by_columns(result, tile)],
        [result],
        cost(2 * tokens * features * width, 2 * (tokens * features + features * width + tokens * width)),
    )[0]


def gelu_parts(value):
    size = jnp.abs(value) * (0.5**0.5)
    near = 1.0 / (1.0 + 0.3275911 * size)
    bell = jnp.exp(-0.5 * value * value)
    series = near * (0.127414796 + near * (-0.142248368 + near * (0.7107068705 + near * (-0.7265760135 + near * 0.5307027145))))
    tail = series * bell
    below = jnp.where(value >= 0, 1.0 - tail, tail)
    return below, value * bell * 0.3989422804014327


def widen_kernel(x_ref, first_ref, second_ref, bias_ref, active_ref, slope_ref):
    depth = first_ref.shape[0]
    for rows in chunks(x_ref.shape[0], ROW_CHUNK):
        total = dot_nn(x_ref[rows, :depth], first_ref[...]) + dot_nn(x_ref[rows, depth:], second_ref[...])
        total = total + bias_ref[...]
        below, slope = gelu_parts(total)
        active_ref[rows, :] = (total * below).astype(jnp.bfloat16)
        slope_ref[rows, :] = (below + slope).astype(jnp.bfloat16)


def feed_in(x, weight, bias, tile, needs=(), through=()):
    tokens, features = x.shape
    width = weight[0].shape[1]
    result = shaped(tokens, width, jnp.bfloat16)
    return run(
        widen_kernel,
        "feed_in",
        (width // tile,),
        (x, *weight, bias),
        [whole(x), by_columns(weight[0], tile), by_columns(weight[1], tile), by_columns(bias, tile)],
        [by_columns(result, tile)] * 2,
        [result] * 2,
        cost(4 * tokens * features * width, 2 * (tokens * features + features * width + 2 * tokens * width)),
        needs,
        through,
    )


def unfeed_kernel(x_ref, first_ref, second_ref, slope_ref, out_ref, sum_ref):
    depth = first_ref.shape[0]
    column_sum = jnp.zeros(sum_ref.shape, jnp.float32)
    for rows in chunks(x_ref.shape[0], ROW_CHUNK):
        total = dot_nn(x_ref[rows, :depth], first_ref[...]) + dot_nn(x_ref[rows, depth:], second_ref[...])
        low = (total * slope_ref[rows, :].astype(jnp.float32)).astype(jnp.bfloat16)
        out_ref[rows, :] = low
        column_sum += jnp.sum(low.astype(jnp.float32), 0, keepdims=True)
    sum_ref[...] = column_sum


def feed_back(x, weight, slope, tile, needs=()):
    tokens, features = x.shape
    width = weight[0].shape[1]
    results = [shaped(tokens, width, jnp.bfloat16), shaped(1, width, jnp.float32)]
    return run(
        unfeed_kernel,
        "feed_back",
        (width // tile,),
        (x, *weight, slope),
        [whole(x), by_columns(weight[0], tile), by_columns(weight[1], tile), by_columns(slope, tile)],
        [by_columns(result, tile) for result in results],
        results,
        cost(2 * tokens * features * width, 2 * (tokens * features + features * width + 2 * tokens * width)),
        needs,
    )


def both_halves(x, first_ref, second_ref):
    return jnp.concatenate([dot_nt(x, first_ref[...]), dot_nt(x, second_ref[...])], 1)


def by_turns(x, first_ref, second_ref, place):
    half = x.shape[1] // 2
    parts = []
    for ref in (first_ref, second_ref):
        near = dot_nt(x[:, :half], ref[:, place * half : (place + 1) * half])
        parts.append(near + dot_nt(x[:, half:], ref[:, (2 + place) * half : (3 + place) * half]))
    return jnp.concatenate(parts, 1)


def layer_norm_rows(summed):
    center = jnp.mean(summed, 1, keepdims=True)
    shifted = summed - center
    inverse = lax.rsqrt(jnp.mean(shifted * shifted, 1, keepdims=True) + epsilon)
    return shifted * inverse, inverse


def layer_norm_back(gradient, normal, inverse, gain):
    scaled = gradient * gain
    first = jnp.mean(scaled, 1, keepdims=True)
    second = jnp.mean(scaled * normal, 1, keepdims=True)
    return inverse * (scaled - first - normal * second)


def attended_kernel(context_ref, first_ref, second_ref, x_ref, vector_ref, normal_ref, low_ref, inverse_ref):
    attended = by_turns(context_ref[...], first_ref, second_ref, 1) + vector_ref[0:1, :]
    normal, inverse = layer_norm_rows(x_ref[...].astype(jnp.float32) + attended)
    normal_ref[...] = normal
    low_ref[...] = (normal * vector_ref[1:2, :] + vector_ref[2:3, :]).astype(jnp.bfloat16)
    inverse_ref[...] = jnp.broadcast_to(inverse, inverse_ref.shape)


def attended_norm(context, weight, x, vectors, tile, needs=(), through=()):
    tokens, features = x.shape
    results = [
        shaped(tokens, features, jnp.float32),
        shaped(tokens, features, jnp.bfloat16),
        shaped(tokens, 128, jnp.float32),
    ]
    return run(
        attended_kernel,
        "attended_norm",
        (tokens // tile,),
        (context, *weight, x, vectors),
        [by_rows(context, tile), whole(weight[0]), whole(weight[1]), by_rows(x, tile), whole(vectors)],
        [by_rows(result, tile) for result in results],
        results,
        cost(2 * tokens * features * context.shape[1], 14 * tokens * features),
        needs,
        through,
    )


def fed_kernel(
    near_ref, far_ref, near0_ref, near1_ref, far0_ref, far1_ref, normal_ref, cotangent_ref, vector_ref, order_ref,
    out_ref, grad_ref, low_ref, sum_ref,
):
    fed = both_halves(near_ref[...], near0_ref, near1_ref) + both_halves(far_ref[...], far0_ref, far1_ref)
    fed = fed + vector_ref[3:4, :]
    hidden = normal_ref[...] * vector_ref[1:2, :] + vector_ref[2:3, :]
    normal, inverse = layer_norm_rows(hidden + fed)
    output = (normal * vector_ref[4:5, :] + vector_ref[5:6, :]).astype(jnp.bfloat16)
    out_ref[...] = dot_nt(output, order_ref[...]).astype(jnp.bfloat16)
    upstream = cotangent_ref[...].astype(jnp.float32)
    gradient = layer_norm_back(upstream, normal, inverse, vector_ref[4:5, :])
    grad_ref[...] = gradient
    low = gradient.astype(jnp.bfloat16)
    low_ref[...] = low

    @pl.when(pl.program_id(0) == 0)
    def clear():
        sum_ref[...] = jnp.zeros_like(sum_ref)

    sum_ref[0:1, :] += jnp.sum(upstream * normal, 0, keepdims=True)
    sum_ref[1:2, :] += jnp.sum(upstream, 0, keepdims=True)
    sum_ref[2:3, :] += jnp.sum(low.astype(jnp.float32), 0, keepdims=True)


def fed_norm(actives, weights, normal, cotangent, vectors, order, tile):
    tokens, features = normal.shape
    halves = [half for weight in weights for half in weight]
    results = [
        shaped(tokens, features, jnp.bfloat16),
        shaped(tokens, features, jnp.float32),
        shaped(tokens, features, jnp.bfloat16),
    ]
    sums = shaped(8, features, jnp.float32)
    units = 2 * actives[0].shape[1]
    return run(
        fed_kernel,
        "fed_norm",
        (tokens // tile,),
        (*actives, *halves, normal, cotangent, vectors, order),
        [by_rows(active, tile) for active in actives]
        + [whole(half) for half in halves]
        + [by_rows(normal, tile), by_rows(cotangent, tile), whole(vectors), whole(order)],
        [by_rows(result, tile) for result in results] + [whole(sums)],
        results + [sums],
        cost(2 * tokens * features * (units + features), 2 * units * (tokens + features) + 14 * tokens * features),
    )


def hidden_kernel(
    near_ref, far_ref, near0_ref, near1_ref, far0_ref, far1_ref, second_grad_ref, normal_ref, inverse_ref, vector_ref,
    grad_ref, low_ref, sum_ref,
):
    gradient = both_halves(near_ref[...], near0_ref, near1_ref) + both_halves(far_ref[...], far0_ref, far1_ref)
    gradient = gradient + second_grad_ref[...]
    normal = normal_ref[...]
    first = layer_norm_back(gradient, normal, inverse_ref[:, 0:1], vector_ref[1:2, :])
    grad_ref[...] = first
    low = first.astype(jnp.bfloat16)
    low_ref[...] = low

    @pl.when(pl.program_id(0) == 0)
    def clear():
        sum_ref[...] = jnp.zeros_like(sum_ref)

    sum_ref[0:1, :] += jnp.sum(gradient * normal, 0, keepdims=True)
    sum_ref[1:2, :] += jnp.sum(gradient, 0, keepdims=True)
    sum_ref[2:3, :] += jnp.sum(low.astype(jnp.float32), 0, keepdims=True)


def hidden_back(pre_grads, weights, second_grad, normal, inverse, vectors, tile, needs=()):
    tokens, features = normal.shape
    halves = [half for weight in weights for half in weight]
    results = [shaped(tokens, features, jnp.float32), shaped(tokens, features, jnp.bfloat16)]
    sums = shaped(8, features, jnp.float32)
    units = 2 * pre_grads[0].shape[1]
    return run(
        hidden_kernel,
        "hidden_back",
        (tokens // tile,),
        (*pre_grads, *halves, second_grad, normal, inverse, vectors),
        [by_rows(pre_grad, tile) for pre_grad in pre_grads]
        + [whole(half) for half in halves]
        + [by_rows(second_grad, tile), by_rows(normal, tile), by_rows(inverse, tile), whole(vectors)],
        [by_rows(result, tile) for result in results] + [whole(sums)],
        results + [sums],
        cost(2 * tokens * features * units, 2 * units * (tokens + features) + 14 * tokens * features),
        needs,
    )


def tokens_kernel(dq_ref, dk_ref, dv_ref, qk0_ref, qk1_ref, vo0_ref, vo1_ref, first_ref, order_ref, out_ref):
    total = (
        by_turns(dq_ref[...], qk0_ref, qk1_ref, 0)
        + by_turns(dk_ref[...], qk0_ref, qk1_ref, 1)
        + by_turns(dv_ref[...], vo0_ref, vo1_ref, 0)
        + first_ref[...]
    )
    out_ref[...] = dot_nt(total.astype(jnp.bfloat16), order_ref[...]).astype(jnp.bfloat16)


def tokens_back(grads, weights, first_grad, order, tile, needs=()):
    tokens, features = first_grad.shape
    halves = [half for weight in weights for half in weight]
    result = shaped(tokens, features, jnp.bfloat16)
    return run(
        tokens_kernel,
        "tokens_back",
        (tokens // tile,),
        (*grads, *halves, first_grad, order),
        [by_rows(grad, tile) for grad in grads]
        + [whole(half) for half in halves]
        + [by_rows(first_grad, tile), whole(order)],
        [by_rows(result, tile)],
        [result],
        cost(8 * tokens * features * features, 20 * tokens * features),
        needs,
    )


def key_bias(length, keys):
    place = lax.broadcasted_iota(jnp.int32, (keys, 1), 0)
    return jnp.where(place < length, 0.0, masked_score)


def attend_kernel(length_ref, q_ref, k_ref, v_ref, context_ref, logsum_ref):
    bias = key_bias(length_ref[pl.program_id(0)], k_ref.shape[0])
    queries = q_ref[...] * (HEAD_DIM**-0.5)
    key_rows = k_ref[...]
    values = v_ref[...].T
    lane = lax.broadcasted_iota(jnp.int32, queries.shape, 1) // HEAD_DIM
    parts = []
    for head in range(queries.shape[1] // HEAD_DIM):
        one = jnp.where(lane == head, queries, jnp.zeros_like(queries))
        scores = dot_nt(key_rows, one) + bias
        top = jnp.max(scores, 0, keepdims=True)
        raised = jnp.exp(scores - top)
        total = jnp.sum(raised, 0, keepdims=True)
        logsum_ref[0, head : head + 1, :] = top + jnp.log(total)
        mixed = dot_nn(values[head * HEAD_DIM : (head + 1) * HEAD_DIM, :], raised.astype(jnp.bfloat16))
        parts.append(mixed / total)
    context_ref[...] = jnp.concatenate(parts, 0).T.astype(jnp.bfloat16)


def attend(queries, key_rows, values, lengths, needs=(), through=()):
    tokens, features = queries.shape
    sequences = lengths.shape[0]
    wide = 2 * HEAD_DIM
    spec = pl.BlockSpec((SEQ_LEN, wide), lambda s, h, _: (s, h))
    steps = features // wide
    return run(
        attend_kernel,
        "attend",
        (sequences, steps),
        (queries, key_rows, values),
        [spec] * 3,
        [spec, pl.BlockSpec((1, 8, SEQ_LEN), lambda s, h, _: (s * steps + h, 0, 0))],
        [shaped(tokens, features, jnp.bfloat16), jax.ShapeDtypeStruct((sequences * steps, 8, SEQ_LEN), jnp.float32)],
        cost(16 * tokens * features * SEQ_LEN, 8 * tokens * features),
        needs,
        through,
        (lengths,),
    )


def attend_back_kernel(length_ref, q_ref, k_ref, v_ref, grad_ref, logsum_ref, dq_ref, dk_ref, dv_ref, sum_ref):
    bias = key_bias(length_ref[pl.program_id(0)], k_ref.shape[0])
    queries = q_ref[...] * (HEAD_DIM**-0.5)
    key_rows = k_ref[...]
    key_columns = key_rows.T
    values = v_ref[...]
    grads = grad_ref[...]
    lane = lax.broadcasted_iota(jnp.int32, queries.shape, 1) // HEAD_DIM
    query_parts = []
    key_grad = jnp.zeros(queries.shape, jnp.float32)
    value_grad = jnp.zeros(queries.shape, jnp.float32)
    for head in range(queries.shape[1] // HEAD_DIM):
        one = jnp.where(lane == head, queries, jnp.zeros_like(queries))
        one_grad = jnp.where(lane == head, grads, jnp.zeros_like(grads))
        chances = jnp.exp(dot_nt(key_rows, one) + bias - logsum_ref[0, head : head + 1, :])
        chance_grad = dot_nt(values, one_grad)
        value_grad += dot_nn(chances.astype(jnp.bfloat16), one_grad)
        inner = jnp.sum(chances * chance_grad, 0, keepdims=True)
        score_grad = (chances * (chance_grad - inner)).astype(jnp.bfloat16)
        key_grad += dot_nn(score_grad, one)
        query_parts.append(dot_nn(key_columns[head * HEAD_DIM : (head + 1) * HEAD_DIM, :], score_grad))
    query_grad = jnp.concatenate(query_parts, 0) * (HEAD_DIM**-0.5)
    query_grad = query_grad.T.astype(jnp.bfloat16)
    value_grad = value_grad.astype(jnp.bfloat16)
    dq_ref[...] = query_grad
    dk_ref[...] = key_grad.astype(jnp.bfloat16)
    dv_ref[...] = value_grad
    sum_ref[...] = jnp.zeros_like(sum_ref)
    sum_ref[0, 0:1, :] = jnp.sum(query_grad.astype(jnp.float32), 0, keepdims=True)
    sum_ref[0, 1:2, :] = jnp.sum(value_grad.astype(jnp.float32), 0, keepdims=True)


def attend_grads(queries, key_rows, values, context_grad, logsums, lengths, part, filled=(), needs=()):
    tokens, features = queries.shape
    sequences = lengths.shape[0]
    wide = 2 * HEAD_DIM
    steps = features // wide
    count = steps // 2
    first = part * count
    spec = pl.BlockSpec((SEQ_LEN, wide), lambda s, h, _: (s, first + h))
    sums_spec = pl.BlockSpec((1, 8, wide), lambda s, h, _: (s, 0, first + h))
    results = [shaped(tokens, features, jnp.bfloat16)] * 3
    results = results + [jax.ShapeDtypeStruct((sequences, 8, features), jnp.float32)]

    def kernel(*refs):
        attend_back_kernel(*refs[:6], *refs[6 + len(filled) :])

    return run(
        kernel,
        "attend_grads",
        (sequences, count),
        (queries, key_rows, values, context_grad, logsums, *filled),
        [spec] * 4
        + [pl.BlockSpec((1, 8, SEQ_LEN), lambda s, h, _: (s * steps + first + h, 0, 0))]
        + [pl.BlockSpec(memory_space=pltpu.HBM)] * len(filled),
        [spec] * 3 + [sums_spec],
        results,
        cost(20 * tokens * features * SEQ_LEN, 7 * tokens * features),
        needs,
        (),
        (lengths,),
        {5 + place: place for place in range(len(filled))},
    )


def weight_grad(left, right):
    half = left.shape[1] // 2

    def part(columns):
        return lax.dot_general(left[:, columns], right, (((0,), (0,)), ((), ())), preferred_element_type=jnp.float32)

    return part(slice(0, half)), part(slice(half, 2 * half)).astype(jnp.bfloat16)


def by_tokens(
    tokens,
    qkv_weight,
    qv_bias,
    out_weight,
    out_bias,
    norm1_gain,
    norm1_shift,
    in_weight,
    in_bias,
    down_weight,
    down_bias,
    norm2_gain,
    norm2_shift,
    lengths,
    cotangent,
):
    rows = lax.axis_size("row")
    row, col = lax.axis_index("row"), lax.axis_index("col")
    local_width = tokens.shape[1]
    features = 2 * local_width
    share = tokens.shape[0] // 2
    bits = [1 << level for level in range(1, rows.bit_length() - 1)]
    cross, line = bits[0], bits[:0:-1]
    via_col = line + [cross, 0]
    via_row = line + [0, cross]

    levels = len(line)
    units = in_weight.shape[1] // 2
    tokens_far = hop(lax.dynamic_slice_in_dim(tokens, (1 - col) * share, share, 0), "col", 1, 2)
    small = jnp.stack([out_bias, norm1_gain, norm1_shift, down_bias, norm2_gain, norm2_shift, qv_bias[0], qv_bias[1]])
    small = jnp.concatenate([small, in_bias.reshape(-1, local_width)], 0)
    qk = Gather(jnp.concatenate([qkv_weight[:, 0], qkv_weight[:, 1]], 1), via_col, rows)
    vo = Gather(jnp.concatenate([qkv_weight[:, 2], out_weight], 1), via_row, rows)
    in_near, in_far = (
        Gather(in_weight[:, :units], via_col, rows),
        Gather(in_weight[:, units:], via_row, rows),
    )
    down_near, down_far = (
        Gather(down_weight[:, :units], via_col, rows),
        Gather(down_weight[:, units:], via_row, rows),
    )
    qk.start()
    vo.start()
    far = hop(small, "col", 1, 2)
    order = order_matrix(row, col, rows, features)
    for step in range(levels - 1):
        order = point(order, [qk, vo], [qk, vo])
    order = point(order, [qk, vo], [qk, vo, in_near, in_far])
    tokens_near = lax.dynamic_slice_in_dim(tokens, col * share, share, 0)
    x = dot_nn(jnp.concatenate([tokens_near, tokens_far], 1), order).astype(jnp.bfloat16)
    for step in range(levels - 1):
        x = point(x, [in_near, in_far], [in_near, in_far])
    x = point(x, [qk, vo], [qk, vo])
    x = point(x, [in_near, in_far], [down_near, down_far])
    for step in range(levels - 1):
        x = point(x, [down_near, down_far], [down_near, down_far])
    x = point(x, [qk, vo], [qk, vo, in_near, in_far])
    qk_full, vo_full = qk.both(), vo.both()

    pair = jnp.concatenate([small, far], 1)
    straight = jnp.where(col == 0, pair[:6], jnp.concatenate([far[:6], small[:6]], 1))
    vectors = jnp.pad(to_relative(straight, row, rows), ((0, 2), (0, 0)))
    in_biases = [
        jnp.concatenate([one.reshape(2, 1, -1)[half] for one in (small[8:], far[8:])], 1) for half in range(2)
    ]
    own_lengths = lax.dynamic_slice_in_dim(lengths, col * (lengths.shape[0] // 2), lengths.shape[0] // 2)
    no_bias = jnp.zeros((1, features), jnp.float32)

    queries = project(x, qk_full, pair[6:7], 0)
    key_rows = project(x, qk_full, no_bias, 1)
    x_last, queries, key_rows = lax.optimization_barrier((x, queries, key_rows))
    values = project(x_last, vo_full, pair[7:8], 0)
    values = point(values, [in_near, in_far, down_near, down_far], [in_near, in_far])
    context, logsums = attend(queries, key_rows, values, own_lengths)
    context = point(context, [in_near, in_far], [in_near, in_far, down_near, down_far])
    cotangent_far = lax.dynamic_slice_in_dim(cotangent, (1 - col) * share, share, 0)
    context, cotangent_far = lax.optimization_barrier((context, cotangent_far))
    cotangent_far = hop(cotangent_far, "col", 1, 2)
    normal_one, hidden_low, inverse_one = attended_norm(context, vo_full, x, vectors, 256)
    in_full = [in_near.both(), in_far.both()]
    active_near, slope_near = feed_in(hidden_low, in_full[0], in_biases[0], 512)
    hidden_low, active_near, cotangent_far = lax.optimization_barrier((hidden_low, active_near, cotangent_far))
    cotangent_near = lax.dynamic_slice_in_dim(cotangent, col * share, share, 0)
    hidden_low = point(hidden_low, [down_near, down_far], [down_near, down_far])
    active_far, slope_far = feed_in(hidden_low, in_full[1], in_biases[1], 512)
    active_far = point(active_far, [down_near, down_far], [down_near, down_far])
    down_full = [down_near.both(), down_far.both()]
    upstream = dot_nn(jnp.concatenate([cotangent_near, cotangent_far], 1), order).astype(jnp.bfloat16)
    output, grad_second, grad_fed, sums_two = fed_norm(
        (active_near, active_far), down_full, normal_one, upstream, vectors, order, 256
    )

    half = local_width
    output_far = hop(output[:, half:], "col", 1, 2)
    back = line[::-1]
    by_cross, by_col = [cross, 0] + back, [0, cross] + back
    down_parts = [weight_grad(grad_fed, active) for active in (active_near, active_far)]
    downs = [Scatter(parts, path, rows) for parts, path in zip(down_parts, (by_cross, by_col))]
    pre_near, sum_near = feed_back(grad_fed, down_full[0], slope_near, 512, [sent for _, sent in down_parts])
    pre_far, sum_far = feed_back(grad_fed, down_full[1], slope_far, 512)
    pre_far, output_far = lax.optimization_barrier((pre_far, output_far))
    pre_far = point(pre_far, downs, downs)
    in_parts = [weight_grad(hidden_low, pre_grad) for pre_grad in (pre_near, pre_far)]
    ins = [Scatter(parts, path, rows) for parts, path in zip(in_parts, (by_cross, by_col))]
    grad_first, grad_attended, sums_one = hidden_back(
        (pre_near, pre_far), in_full, grad_second, normal_one, inverse_one, vectors, 256,
        [down.held for down in downs] + [sent for _, sent in in_parts],
    )
    grad_attended = point(grad_attended, ins + downs, ins + downs)
    out_parts = weight_grad(grad_attended, context)
    outs = [Scatter(out_parts, back + [cross, 0], rows)]
    grad_attended, _ = lax.optimization_barrier((grad_attended, out_parts[1]))
    context_grad = project(grad_attended, vo_full, no_bias, 1)
    context_grad = point(context_grad, outs, outs)
    attention = (queries, key_rows, values)
    near_grads = list(attend_grads(*attention, context_grad, logsums, own_lengths, 1))
    near_grads[0] = point(near_grads[0], outs, outs)
    dq, dk, dv, qv_sums = attend_grads(*attention, context_grad, logsums, own_lengths, 0, near_grads)
    def straighten(array):
        split = array.reshape(array.shape[0], 2, -1)
        return jnp.where(col == 0, split, jnp.flip(split, 1)).reshape(array.shape[0], -1)

    def own(array):
        return lax.dynamic_slice_in_dim(array, col * (array.shape[1] // 2), array.shape[1] // 2, 1)

    feature_sums = from_relative(jnp.concatenate([sums_two[:3], sums_one[:3]], 0), row, rows)
    unit_sums = straighten(jnp.concatenate([sum_near, sum_far], 0))
    qv_sums = straighten(jnp.sum(qv_sums, 0)[:2])
    sums = jnp.concatenate([feature_sums, unit_sums.reshape(-1, features), qv_sums], 0)
    sums = lax.all_gather(sums, ("row", "col"))
    value_parts = weight_grad(x, dv)
    turns = jnp.concatenate([dq[:, :half], dk[:, :half], dq[:, half:], dk[:, half:]], 1)
    pair_parts = weight_grad(x, turns)
    pairs, lone = [Scatter(pair_parts, by_cross, rows)], [Scatter(value_parts, back + [0, cross], rows)]
    dv, _, _ = lax.optimization_barrier((dv, pair_parts[1], value_parts[1]))
    dv = point(dv, ins + downs + outs, ins + downs + outs)
    dv = point(dv, pairs + lone, pairs + lone)
    (tokens_grad,) = tokens_back((dq, dk, dv), (qk_full, vo_full), grad_first, order, 256)
    tokens_grad = point(tokens_grad, pairs, pairs)
    tokens_mine = tokens_grad[:, :half]
    tokens_far = hop(tokens_grad[:, half:], "col", 1, 2)
    later = ins + downs + outs + lone + pairs
    tokens_mine, output_far = lax.optimization_barrier((tokens_mine, output_far))
    tokens_mine = point(tokens_mine, downs + outs + lone, downs + outs + lone)
    tokens_mine = point(tokens_mine, pairs, pairs)
    tokens_mine = point(tokens_mine, ins, ins)
    tokens_mine = point(tokens_mine, pairs, pairs)
    tokens_mine = point(tokens_mine, downs + lone, downs + lone)
    tokens_mine, tokens_far = lax.optimization_barrier((tokens_mine, tokens_far))
    while any(chain.order for chain in later):
        moving = [chain for chain in later if chain.order]
        tokens_mine = point(tokens_mine, moving, [chain for chain in moving if len(chain.order) > 1])
    turned = pairs[0].result()

    def give(mine, arrived):
        return jnp.where(col == 0, jnp.concatenate([mine, arrived], 0), jnp.concatenate([arrived, mine], 0))

    sums, tokens_mine = lax.optimization_barrier((sums, tokens_mine))
    sums = jnp.sum(sums, 0)
    feature_sums = own(sums[:6])
    in_bias_grad = own(sums[6:-2].reshape(2, -1)).reshape(-1)
    return (
        give(output[:, :half], output_far),
        give(tokens_mine, tokens_far).astype(jnp.float32),
        jnp.stack([turned[:, :half], turned[:, half:], lone[0].result()], 1),
        own(sums[-2:]),
        outs[0].result(),
        feature_sums[5],
        feature_sums[3],
        feature_sums[4],
        jnp.concatenate([chain.result() for chain in ins], 1),
        in_bias_grad,
        jnp.concatenate([chain.result() for chain in downs], 1),
        feature_sums[2],
        feature_sums[0],
        feature_sums[1],
    )


def device_program(*arrays):
    rows, cols = lax.axis_size("row"), lax.axis_size("col")
    sequences = arrays[13].shape[0]
    if cols == 2 and rows >= 8 and rows & (rows - 1) == 0 and sequences % 2 == 0:
        return by_tokens(*arrays)
    return on_device(*arrays)


def solution(mesh):
    placed = (
        P("row", "col"),
        P("row", None, "col"),
        P(None, "col"),
        P("row", "col"),
        P("col"),
        P("col"),
        P("col"),
        P("row", "col"),
        P("col"),
        P("row", "col"),
        P("col"),
        P("col"),
        P("col"),
        P("row"),
        P("row", "col"),
    )
    return jax.shard_map(
        device_program,
        mesh=mesh,
        in_specs=placed,
        out_specs=(
            P("row", "col"),
            P("row", "col"),
            P("row", None, "col"),
            P(None, "col"),
            P("row", "col"),
            P("col"),
            P("col"),
            P("col"),
            P("row", "col"),
            P("col"),
            P("row", "col"),
            P("col"),
            P("col"),
            P("col"),
        ),
        check_vma=False,
    )
```
